128 devices in a mesh: dp: 16 (over x, z), pipe: 4 (over y_lo, core), tensor: 2 (over y_hi).
Axes of the slice: x: 4, y: 4 (y_hi: 2, y_lo: 2; y = y_hi * 2 + y_lo), z: 4, core: 2. Of those that a mesh axis runs over, the one named last changes fastest.
Arguments:
- stream: bfloat16 [4, 4096, 8192], P('pipe', 'dp', 'tensor'), as said below
- backup_stream: bfloat16 [4, 4096, 8192], P('pipe', 'dp', 'tensor'), as said below
- norm_gain: float32 [8192], P('tensor'), may hold values from 0.5 to 2
- w_key: bfloat16 [4, 8192, 1024], P('pipe', None, 'tensor'), may hold values from -0.0625 to 0.0625
- w_value: bfloat16 [4, 8192, 1024], P('pipe', None, 'tensor'), may hold values from -0.0625 to 0.0625
- key_cot: bfloat16 [4, 4096, 1024], P('pipe', 'dp', 'tensor'), as said below
- value_cot: bfloat16 [4, 4096, 1024], P('pipe', 'dp', 'tensor'), as said below
- backup_key_cot: bfloat16 [4, 4096, 1024], P('pipe', 'dp', 'tensor'), as said below
- backup_value_cot: bfloat16 [4, 4096, 1024], P('pipe', 'dp', 'tensor'), as said below
- positions: int32 [4, 4096], P('pipe'), may hold values from 0 to 4095, as said below
- failed: int32 [4], replicated, may hold values from 0 to 15, as said below
- reroute_plan: int32 [4, 32], replicated, may hold values from 0 to 15, as said below
Outputs:
- grad_key: float32 [4, 8192, 1024], P('pipe', 'dp', 'tensor')
- grad_value: float32 [4, 8192, 1024], P('pipe', 'dp', 'tensor')
- stream_grad: bfloat16 [4, 4096, 8192], P('pipe', 'dp', 'tensor')
- spill_grad: bfloat16 [4, 768, 8192], P('pipe', 'dp', 'tensor')
The draws below stay inside these ranges and needn't reach their ends.
Inputs may be any that keep to these rules, and one draw needn't show every extreme that they name: failed[s] is the replica of section s that has failed; some section has lost replica 0 and some other section replica 16 - 1. reroute_plan[s, b] never equals failed[s]; every other replica takes at least one block of each section, none more than 6, and some replica takes exactly 6. positions count from 0 at each document start; documents of a section's rows start at least every 4096 rows, and in some section exactly every 4096 rows. In stream[j] the rows of replica failed[(j + 1) mod 4] are zero. In backup_stream[s] only the rows of replica (failed[s] + 1) mod 16 are nonzero. In key_cot[s] the rows of replica failed[s] are zero. In value_cot[s] the rows of replica failed[s] are zero. In backup_key_cot[s] only the rows of replica (failed[s] + 1) mod 16 are nonzero. In backup_value_cot[s] only the rows of replica (failed[s] + 1) mod 16 are nonzero.
All inputs are finite; a program needn't handle non-finite values.
Results may differ from the reference program's by a relative error of at most 0.015.
Values may be sent and summed in bfloat16 or wider, within the bound.
No kernel may reach another device: no remote copies, remote signals or barrier semaphores. Data moves between devices by JAX's collectives and lax.ppermute only.
A program may use at most 128 MiB of HBM per device.

```python
import math
import jax
import jax.numpy as jnp
from jax import lax

D = 8192
KV_HEADS = 8
HEAD = 128
TOK_DEV = 256
BLOCK = 8
SEQ = 4096
TOKENS = 4096
REPLICAS = 16
SECTIONS = 4
BLOCKS = 32
MOST_BLOCKS = 6
SPILL = 48


def plan_parts(key):
    key = jax.random.fold_in(key, 7)
    key_ids, key_pick, key_sections = jax.random.split(key, 3)
    section_ids = jnp.arange(SECTIONS, dtype=jnp.int32)
    drawn_ids = jax.random.randint(key_ids, (SECTIONS,), 0, REPLICAS).astype(jnp.int32)
    marked = jax.random.randint(key_pick, (), 0, SECTIONS).astype(jnp.int32)
    failed_ids = jnp.where(section_ids == marked, REPLICAS - 1, drawn_ids)
    failed_ids = jnp.where(section_ids == (marked + 1) % SECTIONS, 0, failed_ids).astype(jnp.int32)
    section_keys = jax.random.split(key_sections, SECTIONS)
    extra_count = BLOCKS - (REPLICAS - 1) - (MOST_BLOCKS - 1)

    def single_section(section_key, failed_id):
        key_busiest, key_slots, key_shuffle = jax.random.split(section_key, 3)
        busiest = jax.random.randint(key_busiest, (), 0, REPLICAS - 1).astype(jnp.int32)
        every_one = jnp.arange(REPLICAS - 1, dtype=jnp.int32)
        heavy = jnp.full((MOST_BLOCKS - 1,), busiest, dtype=jnp.int32)
        slot_pick = jax.random.permutation(key_slots, (REPLICAS - 2) * (MOST_BLOCKS - 1))[:extra_count]
        remaining = (slot_pick // (MOST_BLOCKS - 1)).astype(jnp.int32)
        remaining = remaining + jnp.where(remaining >= busiest, 1, 0).astype(jnp.int32)
        chosen = jnp.concatenate([every_one, heavy, remaining])
        shuffle = jax.random.permutation(key_shuffle, BLOCKS)
        chosen = chosen[shuffle]
        replica = chosen + jnp.where(chosen >= failed_id, 1, 0).astype(jnp.int32)
        return replica.astype(jnp.int32)
    plans = jax.vmap(single_section)(section_keys, failed_ids)
    return (failed_ids, plans)


def row_owner():
    return jnp.arange(TOKENS, dtype=jnp.int32) // TOK_DEV


def stream_field(key, rise_top):
    key = jax.random.fold_in(key, 13)
    key_base = jax.random.fold_in(key, 0)
    key_row = jax.random.fold_in(key, 2)
    key_col = jax.random.fold_in(key, 3)
    shape = (SECTIONS, TOKENS, D)
    column = jnp.arange(D, dtype=jnp.float32)[None, None, :] / (D - 1)
    base = jax.random.normal(key_base, shape, jnp.float32)
    rise = jnp.exp(column * math.log(rise_top))
    row_scale = jnp.exp(jax.random.uniform(key_row, (SECTIONS, TOKENS, 1), jnp.float32, math.log(0.02), math.log(0.2)))
    col_scale = jnp.exp(jax.random.uniform(key_col, (1, 1, D), jnp.float32, 0.0, math.log(10.0)))
    return base * row_scale * col_scale * rise


def cot_field(key, salt):
    key = jax.random.fold_in(key, salt)
    key_normal = jax.random.fold_in(key, 0)
    shape = (SECTIONS, TOKENS, KV_HEADS * HEAD)
    normal_part = jnp.clip(0.1 * jax.random.normal(key_normal, shape, jnp.float32), -0.6, 0.6)
    return normal_part


def drop_failed(field, failed_ids):
    live = row_owner()[None, :] != failed_ids[:, None]
    return jnp.where(live[:, :, None], field, 0.0)


def keep_saved(field, failed_ids):
    moved = jnp.roll(field, TOK_DEV, axis=1)
    keeper = (failed_ids + 1) % REPLICAS
    held = row_owner()[None, :] == keeper[:, None]
    return jnp.where(held[:, :, None], moved, 0.0)


def draw_failed(key, part):
    return plan_parts(key)[0]


def draw_reroute_plan(key, part):
    return plan_parts(key)[1]


def draw_positions(key, part):
    key = jax.random.fold_in(key, 11)
    key_bound, key_quiet = jax.random.split(key, 2)
    quiet = jax.random.randint(key_quiet, (), 0, SECTIONS).astype(jnp.int32)
    section_ids = jnp.arange(SECTIONS, dtype=jnp.int32)[:, None]
    boundary = (jax.random.randint(key_bound, (SECTIONS, TOKENS), 0, 512) == 0) & (section_ids != quiet)
    places = jnp.arange(TOKENS, dtype=jnp.int32)[None, :] + jnp.zeros((SECTIONS, 1), jnp.int32)
    starts = jnp.where(boundary | (places % SEQ == 0), places, 0)
    doc_start = lax.cummax(starts, axis=1)
    return (places - doc_start).astype(jnp.int32)


def draw_stream(key, part):
    field = stream_field(key, 4.0)
    failed_ids = plan_parts(key)[0]
    return drop_failed(field, jnp.roll(failed_ids, -1)).astype(jnp.bfloat16)


def draw_backup_stream(key, part):
    field = stream_field(key, 4.0)
    failed_ids = plan_parts(key)[0]
    return keep_saved(jnp.roll(field, 1, axis=0), failed_ids).astype(jnp.bfloat16)


def draw_key_cot(key, part):
    field = cot_field(key, 17)
    return drop_failed(field, plan_parts(key)[0]).astype(jnp.bfloat16)


def draw_backup_key_cot(key, part):
    field = cot_field(key, 17)
    return keep_saved(field, plan_parts(key)[0]).astype(jnp.bfloat16)


def draw_value_cot(key, part):
    field = cot_field(key, 19)
    return drop_failed(field, plan_parts(key)[0]).astype(jnp.bfloat16)


def draw_backup_value_cot(key, part):
    field = cot_field(key, 19)
    return keep_saved(field, plan_parts(key)[0]).astype(jnp.bfloat16)


def shard_levels(rng, extent, cuts, least, top_value):
    def one(dim, parts):
        heights = jax.random.uniform(jax.random.fold_in(jax.random.fold_in(rng, 6), dim), (parts,), jnp.float32, least / len(cuts), top_value / len(cuts))
        return jnp.repeat(jnp.exp(heights), extent[dim] // parts).reshape((-1,) + (1,) * (len(extent) - dim - 1))

    loudness = one(*cuts[0])
    for cut in cuts[1:]:
        loudness = loudness * one(*cut)
    return loudness


def normal_values(own_key, shape, width, bound, cuts=(), kind=jnp.bfloat16):
    level = shard_levels(own_key, shape, cuts, -0.22, 0.18) if cuts else 1.0
    entries = jax.random.normal(own_key, shape, jnp.float32) * width * level
    return jnp.minimum(jnp.maximum(entries, -bound), bound).astype(kind)


def setup_inputs(seed: int = 0) -> dict:
    arg_keys = jax.random.split(jax.random.key(seed), 13)
    stream = draw_stream(jax.random.fold_in(arg_keys[12], 71), 0)
    backup_stream = draw_backup_stream(jax.random.fold_in(arg_keys[12], 71), 0)
    norm_gain = jnp.clip(jnp.exp(math.log(2.0) - 1.3862944 * jax.random.uniform(arg_keys[2], (D,), jnp.float32) ** shard_levels(arg_keys[2], (D,), ((0, 2),), -0.2, 0.2)), 0.5, 2.0)
    w_key = normal_values(arg_keys[3], (SECTIONS, D, KV_HEADS * HEAD), D ** -0.5, 0.0625, ((0, 4), (2, 2)))
    w_value = normal_values(arg_keys[4], (SECTIONS, D, KV_HEADS * HEAD), D ** -0.5, 0.0625, ((0, 4), (2, 2)))
    key_cot = draw_key_cot(jax.random.fold_in(arg_keys[12], 71), 0)
    value_cot = draw_value_cot(jax.random.fold_in(arg_keys[12], 71), 0)
    backup_key_cot = draw_backup_key_cot(jax.random.fold_in(arg_keys[12], 71), 0)
    backup_value_cot = draw_backup_value_cot(jax.random.fold_in(arg_keys[12], 71), 0)
    positions = draw_positions(jax.random.fold_in(arg_keys[12], 71), 0)
    failed = draw_failed(jax.random.fold_in(arg_keys[12], 71), 0)
    reroute_plan = draw_reroute_plan(jax.random.fold_in(arg_keys[12], 71), 0)
    return dict(stream=stream, backup_stream=backup_stream, norm_gain=norm_gain, w_key=w_key, w_value=w_value, key_cot=key_cot, value_cot=value_cot, backup_key_cot=backup_key_cot, backup_value_cot=backup_value_cot, positions=positions, failed=failed, reroute_plan=reroute_plan)


EPSILON = 1e-05
ROPE_BASE = 500000.0

def frequencies():
    index_half = jnp.arange(HEAD // 2, dtype=jnp.float32)
    return jnp.exp(-(2.0 * index_half / HEAD) * math.log(ROPE_BASE))

def derotate(cotangent, position):
    row_count = cotangent.shape[0]
    pieces = cotangent.astype(jnp.float32).reshape(row_count, -1, 2, HEAD // 2)
    angles = position.astype(jnp.float32)[:, None] * frequencies()[None, :]
    cosine = jnp.cos(angles)[:, None, :]
    sine_values = jnp.sin(angles)[:, None, :]
    lower_half = pieces[:, :, 0, :]
    upper_half = pieces[:, :, 1, :]
    new_lower = lower_half * cosine + upper_half * sine_values
    new_upper = upper_half * cosine - lower_half * sine_values
    return jnp.stack([new_lower, new_upper], axis=2).reshape(row_count, -1).astype(jnp.bfloat16)

def slot_rows(plan_row, owners, capacity_blocks, block_size):
    block_count = plan_row.shape[0]
    block_ids = jnp.arange(block_count, dtype=jnp.int32)
    same_owner = plan_row[:, None] == plan_row[None, :]
    earlier = block_ids[None, :] < block_ids[:, None]
    block_rank = lax.optimization_barrier(jnp.sum(jnp.where(same_owner & earlier, 1, 0), axis=1)).astype(jnp.int32)
    slot_ids = jnp.arange(capacity_blocks, dtype=jnp.int32)
    matches = (plan_row[None, None, :] == owners[:, None, None]) & (block_rank[None, None, :] == slot_ids[None, :, None])
    chosen = lax.optimization_barrier(jnp.sum(jnp.where(matches, block_ids[None, None, :], 0), axis=2)).astype(jnp.int32)
    filled = jnp.any(matches, axis=2)
    offsets = jnp.arange(block_size, dtype=jnp.int32)
    indices = (chosen[:, :, None] * block_size + offsets[None, None, :]).reshape(owners.shape[0], -1)
    occupied = jnp.repeat(filled, block_size, axis=1)
    return (indices, occupied)

def restore(current, saved, dead_start, saved_start):
    saved_rows = lax.dynamic_slice_in_dim(saved, saved_start, TOK_DEV, 0)
    return lax.dynamic_update_slice_in_dim(current, saved_rows, dead_start, 0)

def reference(stream, backup_stream, norm_gain, w_key, w_value, key_cot, value_cot, backup_key_cot, backup_value_cot, positions, failed, reroute_plan):
    key_width = KV_HEADS * HEAD
    owners = jnp.arange(REPLICAS, dtype=jnp.int32)
    grads_key = []
    grads_value = []
    stream_out = [None] * SECTIONS
    spill_out = [None] * SECTIONS
    for section_idx in range(SECTIONS):
        source = (section_idx - 1) % SECTIONS
        fallen = failed[section_idx].astype(jnp.int32)
        keeper = ((fallen + 1) % REPLICAS).astype(jnp.int32)
        dead_start = (fallen * TOK_DEV).astype(jnp.int32)
        saved_start = (keeper * TOK_DEV).astype(jnp.int32)
        full_stream = restore(stream[source], backup_stream[section_idx], dead_start, saved_start)
        full_key = restore(key_cot[section_idx], backup_key_cot[section_idx], dead_start, saved_start)
        full_value = restore(value_cot[section_idx], backup_value_cot[section_idx], dead_start, saved_start)
        values = full_stream.astype(jnp.float32)
        scales = lax.rsqrt(lax.optimization_barrier(jnp.mean(values * values, axis=1)) + EPSILON)
        normed = (values * scales[:, None] * norm_gain).astype(jnp.bfloat16)
        cot_key = derotate(full_key, positions[section_idx])
        cots = jnp.concatenate([cot_key, full_value], axis=1)
        feature = jnp.dot(cot_key, w_key[section_idx].T, preferred_element_type=jnp.float32)
        feature = feature + jnp.dot(full_value, w_value[section_idx].T, preferred_element_type=jnp.float32)
        scaled = norm_gain * feature
        input_grad = (scales[:, None] * scaled).astype(jnp.bfloat16)
        replica = jnp.arange(TOKENS, dtype=jnp.int32) // TOK_DEV
        live_rows = (replica != fallen)[:, None]
        stream_out[source] = jnp.where(live_rows, input_grad, jnp.zeros((), jnp.bfloat16))
        indices, occupied = slot_rows(reroute_plan[section_idx], owners, SPILL // BLOCK, BLOCK)
        dead_grad = lax.dynamic_slice_in_dim(input_grad, dead_start, TOK_DEV, 0)
        flat_index = indices.reshape(-1)
        flat_occupied = occupied.reshape(-1)[:, None]
        spill_out[source] = jnp.where(flat_occupied, dead_grad[flat_index], jnp.zeros((), jnp.bfloat16))
        dead_normed = lax.dynamic_slice_in_dim(normed, dead_start, TOK_DEV, 0)
        dead_cots = lax.dynamic_slice_in_dim(cots, dead_start, TOK_DEV, 0)
        masked_normed = jnp.where(live_rows, normed, jnp.zeros((), jnp.bfloat16))
        masked_cots = jnp.where(live_rows, cots, jnp.zeros((), jnp.bfloat16))

        def accumulate(running, owner_id):
            own_start = (owner_id * TOK_DEV).astype(jnp.int32)
            own_normed = lax.dynamic_slice_in_dim(masked_normed, own_start, TOK_DEV, 0)
            own_cots = lax.dynamic_slice_in_dim(masked_cots, own_start, TOK_DEV, 0)
            slot_index = indices[owner_id]
            slot_live = occupied[owner_id][:, None]
            far_normed = jnp.where(slot_live, dead_normed[slot_index], jnp.zeros((), jnp.bfloat16))
            far_cots = jnp.where(slot_live, dead_cots[slot_index], jnp.zeros((), jnp.bfloat16))
            rows_normed = jnp.concatenate([own_normed, far_normed], axis=0)
            rows_cots = jnp.concatenate([own_cots, far_cots], axis=0)
            partial_value = lax.dot_general(rows_normed, rows_cots, (((0,), (0,)), ((), ())), preferred_element_type=jnp.float32)
            rounded = lax.optimization_barrier(partial_value.astype(jnp.bfloat16))
            return (running + rounded.astype(jnp.float32), None)
        summed, _ = lax.scan(accumulate, jnp.zeros((D, 2 * key_width), jnp.float32), owners)
        grads_key.append(summed[:, :key_width])
        grads_value.append(summed[:, key_width:])
    return (jnp.stack(grads_key), jnp.stack(grads_value), jnp.stack(stream_out), jnp.stack(spill_out))
```

```python
import itertools
import math

import jax
import jax.numpy as jnp
from jax import lax
from jax.experimental import pallas as pl
from jax.experimental.pallas import tpu as pltpu
from jax.sharding import PartitionSpec as P

D = 8192
HEAD = 128
BLOCK = 8
RING = 4
SECTIONS = 4

EPSILON = 1e-05
ROPE_BASE = 500000.0

AXES = ("dp", "pipe", "tensor")


def moved(block, rule):
    route = []
    for x, z, s, t in itertools.product(range(RING), range(RING), range(SECTIONS), range(2)):
        target = rule(x, z, s, t)
        if target is not None:
            a, b, c, d = target
            there = ((a % RING * RING + b % RING) * SECTIONS + c % SECTIONS) * 2 + d % 2
            route.append((((x * RING + z) * SECTIONS + s) * 2 + t, there))
    return lax.ppermute(block, AXES, route)


def frequencies():
    index_half = jnp.arange(HEAD // 2, dtype=jnp.float32)
    return jnp.exp(-(2.0 * index_half / HEAD) * math.log(ROPE_BASE))


def derotate(cotangent, position):
    row_count = cotangent.shape[0]
    pieces = cotangent.astype(jnp.float32).reshape(row_count, -1, 2, HEAD // 2)
    angles = position.astype(jnp.float32)[:, None] * frequencies()[None, :]
    cosine = jnp.cos(angles)[:, None, :]
    sine_values = jnp.sin(angles)[:, None, :]
    lower_half = pieces[:, :, 0, :]
    upper_half = pieces[:, :, 1, :]
    new_lower = lower_half * cosine + upper_half * sine_values
    new_upper = upper_half * cosine - lower_half * sine_values
    return jnp.stack([new_lower, new_upper], axis=2).reshape(row_count, -1).astype(jnp.bfloat16)


def slot_selection(plan_row, owner, capacity_blocks, rows):
    block_count = plan_row.shape[0]
    block_ids = jnp.arange(block_count, dtype=jnp.int32)
    same_owner = plan_row[:, None] == plan_row[None, :]
    earlier = block_ids[None, :] < block_ids[:, None]
    block_rank = jnp.sum(jnp.where(same_owner & earlier, 1, 0), axis=1).astype(jnp.int32)
    slot_of_block = jnp.where(plan_row == owner, block_rank, -1)
    slot_of_row = jnp.repeat(slot_of_block, BLOCK) * BLOCK + jnp.tile(
        jnp.arange(BLOCK, dtype=jnp.int32), block_count
    )
    slot_of_row = jnp.where(jnp.repeat(slot_of_block, BLOCK) < 0, -1, slot_of_row)
    slot_ids = jnp.arange(capacity_blocks * BLOCK, dtype=jnp.int32)
    return (slot_ids[:, None] == slot_of_row[None, :]).astype(jnp.bfloat16)


NT = (((1,), (1,)), ((), ()))
TN = (((0,), (0,)), ((), ()))
TILE = 1024


def feature_kernel(half, cots, scale, w_key, w_value, out):
    width = w_key.shape[1]
    total = lax.dot_general(cots[:, :width], w_key[...], NT, preferred_element_type=jnp.float32)
    total = total + lax.dot_general(
        cots[:, width:], w_value[...], NT, preferred_element_type=jnp.float32
    )
    out[...] = (total * scale[...]).astype(out.dtype)


def feature_half(cots, scale, w_key, w_value, half):
    rows = cots.shape[0]
    tiles = D // 2 // TILE
    width = w_key.shape[1]
    weights = pl.BlockSpec((TILE, width), lambda i, half: (half[0] * tiles + i, 0))
    return pl.pallas_call(
        feature_kernel,
        out_shape=jax.ShapeDtypeStruct((rows, D // 2), jnp.bfloat16),
        grid_spec=pltpu.PrefetchScalarGridSpec(
            num_scalar_prefetch=1,
            grid=(tiles,),
            in_specs=[
                pl.BlockSpec((rows, 2 * width), lambda i, half: (0, 0)),
                pl.BlockSpec((rows, 1), lambda i, half: (0, 0)),
                weights,
                weights,
            ],
            out_specs=pl.BlockSpec((rows, TILE), lambda i, half: (0, i)),
        ),
        compiler_params=pltpu.CompilerParams(vmem_limit_bytes=32 * 1024 * 1024),
    )(jnp.reshape(half, (1,)), cots, scale, w_key, w_value)


def on_device(
    stream,
    backup_stream,
    norm_gain,
    w_key,
    w_value,
    key_cot,
    value_cot,
    backup_key_cot,
    backup_value_cot,
    positions,
    failed,
    reroute_plan,
):
    section = lax.axis_index("pipe")
    member = lax.axis_index("dp")
    side = lax.axis_index("tensor")
    replicas = lax.axis_size("dp")
    at_x, at_z = member // RING, member % RING
    fallen = failed[section]
    keeper = (fallen + 1) % replicas
    plan_row = reroute_plan[section]
    rows = stream.shape[1]
    capacity_blocks = 2 * ((plan_row.shape[0] + replicas - 2) // (replicas - 1))
    width = w_key.shape[2]

    own_positions = lax.dynamic_slice_in_dim(positions[0], member * rows, rows, 0)
    dead_positions = lax.dynamic_slice_in_dim(positions[0], fallen * rows, rows, 0)
    cot_key = derotate(key_cot[0], own_positions)
    cot_value = value_cot[0]

    def to_stream(block):
        straight = moved(block, lambda x, z, s, t: (x, z, s - 1, t))
        across = moved(block, lambda x, z, s, t: (x, z, s - 1, 1 - t))
        return straight, across

    far_key = jnp.concatenate(to_stream(cot_key), axis=1)
    far_value = jnp.concatenate(to_stream(cot_value), axis=1)

    values = stream[0].astype(jnp.float32)
    saved = backup_stream[0].astype(jnp.float32)
    squares = jnp.concatenate([jnp.sum(values * values, axis=1), jnp.sum(saved * saved, axis=1)])
    scales = lax.rsqrt(lax.psum(squares, "tensor") / D + EPSILON)
    own_scale, saved_scale = scales[:rows, None], scales[rows:, None]
    normed = (values * own_scale * norm_gain).astype(jnp.bfloat16)
    saved_normed = (saved * saved_scale * norm_gain).astype(jnp.bfloat16)

    held_scale = jnp.where(member == keeper, saved_scale, 0.0)
    scale_high = held_scale.astype(jnp.bfloat16)
    scale_low = (held_scale - scale_high.astype(jnp.float32)).astype(jnp.bfloat16)
    saved_cots = jnp.concatenate(
        [
            derotate(backup_key_cot[0], dead_positions),
            backup_value_cot[0],
            jnp.broadcast_to(scale_high, (rows, HEAD)),
            jnp.broadcast_to(scale_low, (rows, HEAD)),
        ],
        axis=1,
    )
    dead_normed, dead_cots = lax.psum((saved_normed, saved_cots), "dp")

    cots = jnp.concatenate([cot_key, cot_value], axis=1)
    ones = jnp.ones((rows, 1), jnp.float32)
    across = feature_half(cots, ones, w_key[0], w_value[0], 1 - side)
    straight = feature_half(cots, ones, w_key[0], w_value[0], side)
    across = moved(across, lambda x, z, s, t: (x, z, s - 1, 1 - t))
    straight = moved(straight, lambda x, z, s, t: (x, z, s - 1, t))
    feature = straight.astype(jnp.float32) + across.astype(jnp.float32)
    stream_grad = (own_scale * (norm_gain * feature)).astype(jnp.bfloat16)

    fourth = normed.shape[1] // RING
    block = fourth // 2

    def along_x(tile, step):
        return moved(tile, lambda x, z, s, t: (x + step, z, s, t)) if step else tile

    def along_z(tile, step):
        return moved(tile, lambda x, z, s, t: (x, z + step, s, t)) if step else tile

    def reduced(piece_of, half_of, head_of, far_cots, at_gather, at_reduce, gather, reduce):
        lhs, rhs = [], []
        for step in range(RING):
            lhs.append(gather(piece_of((at_gather + step) % RING), step))
            rhs.append(gather(far_cots, step))
        lhs, rhs = jnp.concatenate(lhs, axis=0), jnp.concatenate(rhs, axis=0)
        total = None
        for step in (2, 1, 3, 0):
            there = (at_reduce + step) % RING
            part = lax.dot_general(
                lax.dynamic_slice_in_dim(lhs, half_of(there) * block, block, 1),
                lax.dynamic_slice_in_dim(rhs, head_of(there) * width, width, 1),
                TN,
                preferred_element_type=jnp.float32,
            )
            part = reduce(part.astype(jnp.bfloat16), step).astype(jnp.float32)
            total = part if total is None else total + part
        return total.astype(jnp.bfloat16)

    key_blocks = normed.reshape(rows, 2, RING, block)
    grad_key = reduced(
        lambda z: lax.dynamic_index_in_dim(key_blocks, z, 2, keepdims=False).reshape(rows, fourth),
        lambda x: x % 2,
        lambda x: (x // 2) ^ side,
        far_key,
        at_z,
        at_x,
        along_z,
        along_x,
    )
    grad_key = moved(grad_key, lambda x, z, s, t: (2 * t + x % 2, z, s + 1, x // 2))
    grad_value = reduced(
        lambda x: lax.dynamic_slice_in_dim(normed, (2 * (x % 2) + x // 2) * fourth, fourth, 1),
        lambda z: z % 2,
        lambda z: (z // 2) ^ (at_x // 2),
        far_value,
        at_x,
        at_z,
        along_x,
        along_z,
    )
    grad_value = moved(
        grad_value,
        lambda x, z, s, t: (2 * t + x % 2, 2 * (x // 2) + z % 2, s + 1, t ^ (z // 2) ^ (x // 2)),
    )

    home = member // (replicas // 2)
    dead_block = lax.dynamic_slice_in_dim(
        dead_normed, (member % (replicas // 2)) * block, block, 1
    )
    lent = moved(
        dead_block, lambda x, z, s, t: (x, z, s, 1 - t) if t == x // 2 else None
    )
    dead_block = jnp.where(home == side, dead_block, lent)
    dead_part = lax.dot_general(
        dead_block, dead_cots[:, : 2 * width], TN, preferred_element_type=jnp.float32
    )
    grad_key = grad_key.astype(jnp.float32) + dead_part[:, :width]
    grad_value = grad_value.astype(jnp.float32) + dead_part[:, width:]

    selection = slot_selection(plan_row, member, capacity_blocks, rows)
    slots = jnp.dot(selection, dead_cots, preferred_element_type=jnp.float32)
    slot_scale = slots[:, 2 * width : 2 * width + 1] + slots[:, 2 * width + HEAD : 2 * width + HEAD + 1]
    slot_cots = slots[:, : 2 * width].astype(jnp.bfloat16)
    across = feature_half(slot_cots, slot_scale, w_key[0], w_value[0], 1 - side)
    straight = feature_half(slot_cots, slot_scale, w_key[0], w_value[0], side)
    across = moved(across, lambda x, z, s, t: (x, z, s - 1, 1 - t))
    straight = moved(straight, lambda x, z, s, t: (x, z, s - 1, t))
    feature = straight.astype(jnp.float32) + across.astype(jnp.float32)
    spill_grad = (norm_gain * feature).astype(jnp.bfloat16)

    return grad_key[None], grad_value[None], stream_grad[None], spill_grad[None]


def solution(mesh):
    return jax.shard_map(
        on_device,
        mesh=mesh,
        in_specs=(
            P("pipe", "dp", "tensor"),
            P("pipe", "dp", "tensor"),
            P("tensor"),
            P("pipe", None, "tensor"),
            P("pipe", None, "tensor"),
            P("pipe", "dp", "tensor"),
            P("pipe", "dp", "tensor"),
            P("pipe", "dp", "tensor"),
            P("pipe", "dp", "tensor"),
            P("pipe", None),
            P(),
            P(),
        ),
        out_specs=(
            P("pipe", "dp", "tensor"),
            P("pipe", "dp", "tensor"),
            P("pipe", "dp", "tensor"),
            P("pipe", "dp", "tensor"),
        ),
        check_vma=False,
    )
```

```python
import itertools
import math

import jax
import jax.numpy as jnp
from jax import lax
from jax.experimental import pallas as pl
from jax.experimental.pallas import tpu as pltpu
from jax.sharding import PartitionSpec as P

D = 8192
HEAD = 128
BLOCK = 8
RING = 4
SECTIONS = 4

EPSILON = 1e-05
ROPE_BASE = 500000.0

AXES = ("dp", "pipe", "tensor")


def moved(block, rule):
    route = []
    for x, z, s, t in itertools.product(range(RING), range(RING), range(SECTIONS), range(2)):
        target = rule(x, z, s, t)
        if target is not None:
            a, b, c, d = target
            there = ((a % RING * RING + b % RING) * SECTIONS + c % SECTIONS) * 2 + d % 2
            route.append((((x * RING + z) * SECTIONS + s) * 2 + t, there))
    return lax.ppermute(block, AXES, route)


def both_sides(squares):
    return squares + moved(squares, lambda x, z, s, t: (x, z, s, 1 - t))


def frequencies():
    index_half = jnp.arange(HEAD // 2, dtype=jnp.float32)
    return jnp.exp(-(2.0 * index_half / HEAD) * math.log(ROPE_BASE))


def angles_of(position):
    angles = position.astype(jnp.float32)[:, None] * jnp.tile(frequencies(), 2)[None, :]
    sign = jnp.where(jnp.arange(HEAD) < HEAD // 2, 1.0, -1.0)
    return jnp.cos(angles), jnp.sin(angles) * sign


def derotate_kernel(key, value, cosine, sine, out):
    width = key.shape[1]
    for start in range(0, width, HEAD):
        head = key[:, start : start + HEAD].astype(jnp.float32)
        swapped = pltpu.roll(head, HEAD // 2, 1)
        out[:, start : start + HEAD] = (head * cosine[...] + swapped * sine[...]).astype(out.dtype)
    out[:, width:] = value[...]


def derotate(key, value, position):
    cosine, sine = angles_of(position)
    return pl.pallas_call(
        derotate_kernel,
        out_shape=jax.ShapeDtypeStruct((key.shape[0], 2 * key.shape[1]), jnp.bfloat16),
    )(key, value, cosine, sine)


def slot_selection(plan_row, owner, capacity_blocks, rows):
    block_count = plan_row.shape[0]
    block_ids = jnp.arange(block_count, dtype=jnp.int32)
    same_owner = plan_row[:, None] == plan_row[None, :]
    earlier = block_ids[None, :] < block_ids[:, None]
    block_rank = jnp.sum(jnp.where(same_owner & earlier, 1, 0), axis=1).astype(jnp.int32)
    slot_of_block = jnp.where(plan_row == owner, block_rank, -1)
    slot_of_row = jnp.repeat(slot_of_block, BLOCK) * BLOCK + jnp.tile(
        jnp.arange(BLOCK, dtype=jnp.int32), block_count
    )
    slot_of_row = jnp.where(jnp.repeat(slot_of_block, BLOCK) < 0, -1, slot_of_row)
    slot_ids = jnp.arange(capacity_blocks * BLOCK, dtype=jnp.int32)
    return (slot_ids[:, None] == slot_of_row[None, :]).astype(jnp.float32)


NT = (((1,), (1,)), ((), ()))
TN = (((0,), (0,)), ((), ()))
TILE = 1024


def feature_kernel(half, cots, scale, w_key, w_value, across, straight):
    rows, width = cots.shape[0], w_key.shape[1]
    tiles = D // 2 // TILE

    def step(key_tile, value_tile, out):
        total = lax.dot_general(
            cots[:, :width], key_tile[...], NT, preferred_element_type=jnp.float32
        )
        total = total + lax.dot_general(
            cots[:, width:], value_tile[...], NT, preferred_element_type=jnp.float32
        )
        out[...] = (total * scale[...]).astype(out.dtype)

    for side, out in ((1 - half[0], across), (half[0], straight)):
        weights = pl.BlockSpec((TILE, width), lambda i, side=side: (side * tiles + i, 0))
        pltpu.emit_pipeline(
            step,
            grid=(tiles,),
            in_specs=[weights, weights],
            out_specs=[pl.BlockSpec((rows, TILE), lambda i: (0, i))],
        )(w_key, w_value, out)


def feature_halves(cots, scale, w_key, w_value, half):
    rows = cots.shape[0]
    result = jax.ShapeDtypeStruct((rows, D // 2), jnp.bfloat16)
    return pl.pallas_call(
        feature_kernel,
        out_shape=(result, result),
        in_specs=[
            pl.BlockSpec(memory_space=pltpu.SMEM),
            pl.BlockSpec(memory_space=pltpu.VMEM),
            pl.BlockSpec(memory_space=pltpu.VMEM),
            pl.BlockSpec(memory_space=pltpu.HBM),
            pl.BlockSpec(memory_space=pltpu.HBM),
        ],
        out_specs=(pl.BlockSpec(memory_space=pltpu.HBM), pl.BlockSpec(memory_space=pltpu.HBM)),
        compiler_params=pltpu.CompilerParams(vmem_limit_bytes=32 * 1024 * 1024),
    )(
        jnp.reshape(half, (1,)),
        cots,
        scale,
        pltpu.with_memory_space_constraint(w_key, pltpu.HBM),
        pltpu.with_memory_space_constraint(w_value, pltpu.HBM),
    )


def on_device(
    stream,
    backup_stream,
    norm_gain,
    w_key,
    w_value,
    key_cot,
    value_cot,
    backup_key_cot,
    backup_value_cot,
    positions,
    failed,
    reroute_plan,
):
    section = lax.axis_index("pipe")
    member = lax.axis_index("dp")
    side = lax.axis_index("tensor")
    replicas = lax.axis_size("dp")
    at_x, at_z = member // RING, member % RING
    fallen = failed[section]
    plan_row = reroute_plan[section]
    rows = stream.shape[1]
    capacity_blocks = 2 * ((plan_row.shape[0] + replicas - 2) // (replicas - 1))
    width = w_key.shape[2]

    dead_stream, dead_key, dead_value = lax.psum(
        (backup_stream[0], backup_key_cot[0], backup_value_cot[0]), "dp"
    )

    values = stream[0].astype(jnp.float32)
    squares = both_sides(jnp.sum(values * values, axis=1))
    own_scale = lax.rsqrt(squares / D + EPSILON)[:, None]
    normed = (values * own_scale * norm_gain).astype(jnp.bfloat16)

    own_positions = lax.dynamic_slice_in_dim(positions[0], member * rows, rows, 0)
    cots = derotate(key_cot[0], value_cot[0], own_positions)
    near = moved(cots, lambda x, z, s, t: (x, z, s - 1, t))
    far = moved(cots, lambda x, z, s, t: (x, z, s - 1, 1 - t))

    late_cots, normed = lax.optimization_barrier((cots, normed))
    ones = jnp.ones((rows, 1), jnp.float32)
    across, straight = feature_halves(late_cots, ones, w_key[0], w_value[0], side)
    across = moved(across, lambda x, z, s, t: (x, z, s - 1, 1 - t))
    straight = moved(straight, lambda x, z, s, t: (x, z, s - 1, t))
    feature = straight.astype(jnp.float32) + across.astype(jnp.float32)
    stream_grad = (own_scale * (norm_gain * feature)).astype(jnp.bfloat16)

    fourth = normed.shape[1] // RING
    block = fourth // 2
    first = side == 0
    key_heads = [
        jnp.where(first, near[:, :width], far[:, :width]),
        jnp.where(first, far[:, :width], near[:, :width]),
    ]
    outgoing = jnp.stack(
        [
            jnp.concatenate(
                [normed[:, z * block : (z + 1) * block], normed[:, (RING + z) * block : (RING + z + 1) * block]]
                + key_heads,
                axis=1,
            )
            for z in range(RING)
        ]
    )
    z_rings = [[RING * x + z for z in range(RING)] for x in range(RING)]
    x_rings = [[RING * x + z for x in range(RING)] for z in range(RING)]
    arrived = lax.all_to_all(outgoing, "dp", 0, 0, axis_index_groups=z_rings)
    arrived = arrived.reshape(RING * rows, 2 * fourth)

    def product(lhs, rhs):
        return lax.dot_general(lhs, rhs, TN, preferred_element_type=jnp.float32).astype(jnp.bfloat16)

    parts = jnp.stack(
        [
            product(
                arrived[:, half * block : (half + 1) * block],
                arrived[:, fourth + head * width : fourth + (head + 1) * width],
            )
            for head in range(2)
            for half in range(2)
        ]
    )
    parts = lax.all_to_all(parts, "dp", 0, 0, axis_index_groups=x_rings)
    grad_key = jnp.sum(parts.astype(jnp.float32), axis=0).astype(jnp.bfloat16)
    grad_key = moved(grad_key, lambda x, z, s, t: (2 * t + x % 2, z, s + 1, x // 2))

    gathered = []
    for step in (2, 1, 3, 0):
        there = (at_x + step) % RING
        start = (2 * (there % 2) + there // 2) * fourth
        piece = jnp.concatenate(
            [lax.dynamic_slice_in_dim(normed, start, fourth, 1), near[:, width:], far[:, width:]],
            axis=1,
        )
        if step:
            piece = moved(piece, lambda x, z, s, t, step=step: (x + step, z, s, t))
        gathered.append(piece)
    gathered = jnp.concatenate(gathered, axis=0)
    dead_stream, dead_key, dead_value, gathered = lax.optimization_barrier(
        (dead_stream, dead_key, dead_value, gathered)
    )

    total = None
    for step in (2, 1, 3, 0):
        there = (at_z + step) % RING
        half, head = there % 2, (there // 2) ^ (at_x // 2)
        part = product(
            lax.dynamic_slice_in_dim(gathered, half * block, block, 1),
            lax.dynamic_slice_in_dim(gathered, fourth + head * width, width, 1),
        )
        if step:
            part = moved(part, lambda x, z, s, t, step=step: (x, z + step, s, t))
        part = part.astype(jnp.float32)
        total = part if total is None else total + part
    grad_value = moved(
        total.astype(jnp.bfloat16),
        lambda x, z, s, t: (2 * t + x % 2, 2 * (x // 2) + z % 2, s + 1, t ^ (z // 2) ^ (x // 2)),
    )

    dead_values = dead_stream.astype(jnp.float32)
    dead_squares = both_sides(jnp.sum(dead_values * dead_values, axis=1))
    dead_scale = lax.rsqrt(dead_squares / D + EPSILON)[:, None]
    dead_positions = lax.dynamic_slice_in_dim(positions[0], fallen * rows, rows, 0)
    dead_cots = derotate(dead_key, dead_value, dead_positions)

    home = member // (replicas // 2)
    start = (member % (replicas // 2)) * block
    dead_block = (
        lax.dynamic_slice_in_dim(dead_stream, start, block, 1).astype(jnp.float32)
        * dead_scale
        * lax.dynamic_slice_in_dim(norm_gain, start, block, 0)
    ).astype(jnp.bfloat16)
    lent = moved(dead_block, lambda x, z, s, t: (x, z, s, 1 - t) if t == x // 2 else None)
    dead_block = jnp.where(home == side, dead_block, lent)
    dead_part = lax.dot_general(dead_block, dead_cots, TN, preferred_element_type=jnp.float32)
    grad_key = grad_key.astype(jnp.float32) + dead_part[:, :width]
    grad_value = grad_value.astype(jnp.float32) + dead_part[:, width:]

    selection = slot_selection(plan_row, member, capacity_blocks, rows)
    slot_cots = jnp.dot(
        selection.astype(jnp.bfloat16), dead_cots, preferred_element_type=jnp.float32
    ).astype(jnp.bfloat16)
    slot_scale = jnp.sum(selection * jnp.reshape(dead_scale, (1, rows)), axis=1, keepdims=True)
    across, straight = feature_halves(slot_cots, slot_scale, w_key[0], w_value[0], side)
    across = moved(across, lambda x, z, s, t: (x, z, s - 1, 1 - t))
    straight = moved(straight, lambda x, z, s, t: (x, z, s - 1, t))
    feature = straight.astype(jnp.float32) + across.astype(jnp.float32)
    spill_grad = (norm_gain * feature).astype(jnp.bfloat16)

    return grad_key[None], grad_value[None], stream_grad[None], spill_grad[None]


def solution(mesh):
    return jax.shard_map(
        on_device,
        mesh=mesh,
        in_specs=(
            P("pipe", "dp", "tensor"),
            P("pipe", "dp", "tensor"),
            P("tensor"),
            P("pipe", None, "tensor"),
            P("pipe", None, "tensor"),
            P("pipe", "dp", "tensor"),
            P("pipe", "dp", "tensor"),
            P("pipe", "dp", "tensor"),
            P("pipe", "dp", "tensor"),
            P("pipe", None),
            P(),
            P(),
        ),
        out_specs=(
            P("pipe", "dp", "tensor"),
            P("pipe", "dp", "tensor"),
            P("pipe", "dp", "tensor"),
            P("pipe", "dp", "tensor"),
        ),
        check_vma=False,
    )
```

```python
import itertools
import math

import jax
import jax.numpy as jnp
from jax import lax
from jax.experimental import pallas as pl
from jax.experimental.pallas import tpu as pltpu
from jax.sharding import PartitionSpec as P

D = 8192
HEAD = 128
BLOCK = 8
RING = 4
SECTIONS = 4

EPSILON = 1e-05
ROPE_BASE = 500000.0

AXES = ("dp", "pipe", "tensor")


def moved(block, rule):
    route = []
    for x, z, s, t in itertools.product(range(RING), range(RING), range(SECTIONS), range(2)):
        target = rule(x, z, s, t)
        if target is not None:
            a, b, c, d = target
            there = ((a % RING * RING + b % RING) * SECTIONS + c % SECTIONS) * 2 + d % 2
            route.append((((x * RING + z) * SECTIONS + s) * 2 + t, there))
    return lax.ppermute(block, AXES, route)


def both_sides(squares):
    return squares + moved(squares, lambda x, z, s, t: (x, z, s, 1 - t))


def frequencies():
    index_half = jnp.arange(HEAD // 2, dtype=jnp.float32)
    return jnp.exp(-(2.0 * index_half / HEAD) * math.log(ROPE_BASE))


def angles_of(position):
    angles = position.astype(jnp.float32)[:, None] * jnp.tile(frequencies(), 2)[None, :]
    sign = jnp.where(jnp.arange(HEAD) < HEAD // 2, 1.0, -1.0)
    return jnp.cos(angles), jnp.sin(angles) * sign


def derotate_kernel(key, value, cosine, sine, out):
    width = key.shape[1]
    for start in range(0, width, HEAD):
        head = key[:, start : start + HEAD].astype(jnp.float32)
        swapped = pltpu.roll(head, HEAD // 2, 1)
        out[:, start : start + HEAD] = (head * cosine[...] + swapped * sine[...]).astype(out.dtype)
    out[:, width:] = value[...]


def derotate(key, value, position):
    cosine, sine = angles_of(position)
    return pl.pallas_call(
        derotate_kernel,
        out_shape=jax.ShapeDtypeStruct((key.shape[0], 2 * key.shape[1]), jnp.bfloat16),
    )(key, value, cosine, sine)


def slot_selection(plan_row, owner, capacity_blocks, rows):
    block_count = plan_row.shape[0]
    block_ids = jnp.arange(block_count, dtype=jnp.int32)
    same_owner = plan_row[:, None] == plan_row[None, :]
    earlier = block_ids[None, :] < block_ids[:, None]
    block_rank = jnp.sum(jnp.where(same_owner & earlier, 1, 0), axis=1).astype(jnp.int32)
    slot_of_block = jnp.where(plan_row == owner, block_rank, -1)
    slot_of_row = jnp.repeat(slot_of_block, BLOCK) * BLOCK + jnp.tile(
        jnp.arange(BLOCK, dtype=jnp.int32), block_count
    )
    slot_of_row = jnp.where(jnp.repeat(slot_of_block, BLOCK) < 0, -1, slot_of_row)
    slot_ids = jnp.arange(capacity_blocks * BLOCK, dtype=jnp.int32)
    return (slot_ids[:, None] == slot_of_row[None, :]).astype(jnp.float32)


NT = (((1,), (1,)), ((), ()))
TN = (((0,), (0,)), ((), ()))
TILE = 1024


def feature_kernel(half, cots, scale, w_key, w_value, across, straight):
    rows, width = cots.shape[0], w_key.shape[1]
    tiles = D // 2 // TILE

    def step(key_tile, value_tile, out):
        total = lax.dot_general(
            cots[:, :width], key_tile[...], NT, preferred_element_type=jnp.float32
        )
        total = total + lax.dot_general(
            cots[:, width:], value_tile[...], NT, preferred_element_type=jnp.float32
        )
        out[...] = (total * scale[...]).astype(out.dtype)

    for side, out in ((1 - half[0], across), (half[0], straight)):
        weights = pl.BlockSpec((TILE, width), lambda i, side=side: (side * tiles + i, 0))
        pltpu.emit_pipeline(
            step,
            grid=(tiles,),
            in_specs=[weights, weights],
            out_specs=[pl.BlockSpec((rows, TILE), lambda i: (0, i))],
        )(w_key, w_value, out)


def feature_halves(cots, scale, w_key, w_value, half):
    rows = cots.shape[0]
    result = jax.ShapeDtypeStruct((rows, D // 2), jnp.bfloat16)
    return pl.pallas_call(
        feature_kernel,
        out_shape=(result, result),
        in_specs=[
            pl.BlockSpec(memory_space=pltpu.SMEM),
            pl.BlockSpec(memory_space=pltpu.VMEM),
            pl.BlockSpec(memory_space=pltpu.VMEM),
            pl.BlockSpec(memory_space=pltpu.HBM),
            pl.BlockSpec(memory_space=pltpu.HBM),
        ],
        out_specs=(pl.BlockSpec(memory_space=pltpu.HBM), pl.BlockSpec(memory_space=pltpu.HBM)),
        compiler_params=pltpu.CompilerParams(vmem_limit_bytes=32 * 1024 * 1024),
    )(
        jnp.reshape(half, (1,)),
        cots,
        scale,
        pltpu.with_memory_space_constraint(w_key, pltpu.HBM),
        pltpu.with_memory_space_constraint(w_value, pltpu.HBM),
    )


def product_kernel(places, *refs):
    *operands, out = refs
    count = len(operands) // 2
    total = None
    for lhs, rhs in zip(operands[:count], operands[count:]):
        lhs = lhs[...].reshape(-1, lhs.shape[-1])
        rhs = rhs[...].reshape(-1, rhs.shape[-1])
        part = lax.dot_general(lhs, rhs, TN, preferred_element_type=jnp.float32)
        total = part if total is None else total + part
    out[0] = total.astype(out.dtype)


def products(gathered, block, halves, heads):
    left = [
        pl.BlockSpec((g.shape[0], g.shape[1], block), lambda i, at: (0, 0, at[0, i])) for g in gathered
    ]
    right = [
        pl.BlockSpec((g.shape[0], g.shape[1], block), lambda i, at: (0, 0, at[1, i])) for g in gathered
    ]
    places = jnp.stack([jnp.stack(halves), jnp.stack(heads) + 2]).astype(jnp.int32)
    return pl.pallas_call(
        product_kernel,
        out_shape=jax.ShapeDtypeStruct((RING, block, block), jnp.bfloat16),
        grid_spec=pltpu.PrefetchScalarGridSpec(
            num_scalar_prefetch=1,
            grid=(RING,),
            in_specs=left + right,
            out_specs=pl.BlockSpec((1, block, block), lambda i, at: (i, 0, 0)),
        ),
        compiler_params=pltpu.CompilerParams(vmem_limit_bytes=32 * 1024 * 1024),
    )(places, *gathered, *gathered)


def pack_kernel(saved, key, value, out):
    rows, piece = saved.shape
    out[0, :rows, :] = saved[...]
    start = rows
    for source in (key, value):
        for column in range(0, source.shape[1], piece):
            out[0, start : start + source.shape[0], :] = source[:, column : column + piece]
            start += source.shape[0]


def packed(saved, key, value, replicas):
    rows, features = saved.shape
    piece, share, width = features // replicas, rows // replicas, key.shape[1]
    height = rows + 2 * width // piece * share

    def column(i):
        x, z = i // RING, i % RING
        return 2 * (x % 2 * RING + z) + x // 2

    few = pl.BlockSpec((share, width), lambda i: (i, 0))
    return pl.pallas_call(
        pack_kernel,
        out_shape=jax.ShapeDtypeStruct((replicas, height, piece), saved.dtype),
        grid=(replicas,),
        in_specs=[pl.BlockSpec((rows, piece), lambda i: (0, column(i))), few, few],
        out_specs=pl.BlockSpec((1, height, piece), lambda i: (i, 0, 0)),
    )(saved, key, value)


def on_device(
    stream,
    backup_stream,
    norm_gain,
    w_key,
    w_value,
    key_cot,
    value_cot,
    backup_key_cot,
    backup_value_cot,
    positions,
    failed,
    reroute_plan,
):
    section = lax.axis_index("pipe")
    member = lax.axis_index("dp")
    side = lax.axis_index("tensor")
    replicas = lax.axis_size("dp")
    at_x, at_z = member // RING, member % RING
    fallen = failed[section]
    plan_row = reroute_plan[section]
    rows = stream.shape[1]
    capacity_blocks = 2 * ((plan_row.shape[0] + replicas - 2) // (replicas - 1))
    width = w_key.shape[2]

    keeper = (fallen + 1) % replicas
    fourth = stream.shape[2] // RING
    block = fourth // 2
    piece = block // 2
    share = rows // replicas

    saved = backup_stream[0]
    saved_pieces = packed(saved, backup_key_cot[0], backup_value_cot[0], replicas)
    own_positions = lax.dynamic_slice_in_dim(positions[0], member * rows, rows, 0)
    key_first, saved_pieces = lax.optimization_barrier((key_cot[0], saved_pieces))
    cots = derotate(key_first, value_cot[0], own_positions)
    dead = lax.all_to_all(saved_pieces, "dp", 0, 0)
    dead = lax.dynamic_index_in_dim(dead, keeper, 0, keepdims=False)
    near = moved(cots, lambda x, z, s, t: (x, z, s - 1, t))
    far = moved(cots, lambda x, z, s, t: (x, z, s - 1, 1 - t))

    values = stream[0].astype(jnp.float32)
    saved_values = saved.astype(jnp.float32)
    squares = both_sides(
        jnp.concatenate([jnp.sum(values * values, axis=1), jnp.sum(saved_values * saved_values, axis=1)])
    )
    scales = lax.rsqrt(squares / D + EPSILON)
    own_scale = scales[:rows, None]
    normed = (values * own_scale * norm_gain).astype(jnp.bfloat16)

    gathered = []
    for step in (2, 1, 3, 0):
        there = (at_x + step) % RING
        start = (2 * (there % 2) + there // 2) * fourth
        tile = jnp.concatenate(
            [lax.dynamic_slice_in_dim(normed, start, fourth, 1), near[:, width:], far[:, width:]],
            axis=1,
        )
        gathered.append((tile, step))
    first = side == 0
    key_heads = [
        jnp.where(first, near[:, :width], far[:, :width]),
        jnp.where(first, far[:, :width], near[:, :width]),
    ]
    outgoing = jnp.stack(
        [
            jnp.concatenate(
                [normed[:, z * block : (z + 1) * block], normed[:, (RING + z) * block : (RING + z + 1) * block]]
                + key_heads,
                axis=1,
            )
            for z in range(RING)
        ]
    )
    tiles = [tile for tile, _ in gathered]
    outgoing, dead, _ = lax.optimization_barrier((outgoing, dead, tiles))
    gathered = [
        moved(tile, lambda x, z, s, t, step=step: (x + step, z, s, t))[None] if step else tile[None]
        for tile, (_, step) in zip(tiles, gathered)
    ]
    z_rings = [[RING * x + z for z in range(RING)] for x in range(RING)]
    x_rings = [[RING * x + z for x in range(RING)] for z in range(RING)]
    arrived = lax.all_to_all(outgoing, "dp", 0, 0, axis_index_groups=z_rings)

    late_cots, tiles = lax.optimization_barrier((cots, tiles))
    ones = jnp.ones((rows, 1), jnp.float32)
    across, straight = feature_halves(late_cots, ones, w_key[0], w_value[0], side)
    across, straight, dead = lax.optimization_barrier((across, straight, dead))
    across = moved(across, lambda x, z, s, t: (x, z, s - 1, 1 - t))
    straight = moved(straight, lambda x, z, s, t: (x, z, s - 1, t))
    arrived, across, straight = lax.optimization_barrier((arrived, across, straight))
    feature = straight.astype(jnp.float32) + across.astype(jnp.float32)
    stream_grad = (own_scale * (norm_gain * feature)).astype(jnp.bfloat16)

    saved_scale = scales[rows:]
    scale_high = saved_scale.astype(jnp.bfloat16)
    scale_low = (saved_scale - scale_high.astype(jnp.float32)).astype(jnp.bfloat16)
    factors = jnp.concatenate([scale_high.reshape(share, -1), scale_low.reshape(share, -1)], axis=1)
    factors = jnp.pad(factors, ((0, 0), (0, HEAD - factors.shape[1])))
    dead_share = dead[rows:].reshape(-1, share, piece).transpose(1, 0, 2).reshape(share, -1)
    shares = lax.all_gather(jnp.concatenate([dead_share, factors], axis=1), "dp")
    gathered, shares = lax.optimization_barrier((gathered, shares))
    dead_raw = shares[:, :, : 2 * width].reshape(rows, 2 * width)
    factors = lax.dynamic_index_in_dim(shares[:, :, 2 * width :], keeper, 0, keepdims=False)
    factors = factors.astype(jnp.float32)
    dead_scale = (factors[:, :share] + factors[:, share : 2 * share]).reshape(rows)[:, None]
    dead_positions = lax.dynamic_slice_in_dim(positions[0], fallen * rows, rows, 0)
    dead_cots = derotate(dead_raw[:, :width], dead_raw[:, width:], dead_positions)

    start = (at_x % 2 * RING + at_z) * block + at_x // 2 * piece
    dead_piece = (
        dead[:rows].astype(jnp.float32) * dead_scale * lax.dynamic_slice_in_dim(norm_gain, start, piece, 0)
    ).astype(jnp.bfloat16)
    sent = moved(
        dead_piece, lambda x, z, s, t: (x, z, s, 1 - t) if x // 2 == t else (x + 2, z, s, t)
    )
    lent = moved(dead_piece, lambda x, z, s, t: None if x // 2 == t else (x + 2, z, s, 1 - t))
    home = at_x // 2
    same = jnp.where(home == side, dead_piece, sent)
    other = jnp.where(home == side, sent, lent)
    dead_block = jnp.concatenate(
        [jnp.where(home == 0, same, other), jnp.where(home == 0, other, same)], axis=1
    )
    dead_part = lax.dot_general(dead_block, dead_cots, TN, preferred_element_type=jnp.float32)

    steps = (2, 1, 3, 0)
    there = [(at_z + step) % RING for step in steps]
    value_parts = products(
        gathered, block, [r % 2 for r in there], [(r // 2) ^ (at_x // 2) for r in there]
    )
    total = None
    for place, step in enumerate(steps):
        part = value_parts[place]
        if step:
            part = moved(part, lambda x, z, s, t, step=step: (x, z + step, s, t))
        part = part.astype(jnp.float32)
        total = part if total is None else total + part
    grad_value = moved(
        total.astype(jnp.bfloat16),
        lambda x, z, s, t: (2 * t + x % 2, 2 * (x // 2) + z % 2, s + 1, t ^ (z // 2) ^ (x // 2)),
    )
    static = [jnp.int32(r) for r in range(RING)]
    key_parts = products([arrived], block, [r % 2 for r in static], [r // 2 for r in static])
    parts = lax.all_to_all(key_parts, "dp", 0, 0, axis_index_groups=x_rings)
    grad_key = jnp.sum(parts.astype(jnp.float32), axis=0).astype(jnp.bfloat16)
    grad_key = moved(grad_key, lambda x, z, s, t: (2 * t + x % 2, z, s + 1, x // 2))
    grad_key = grad_key.astype(jnp.float32) + dead_part[:, :width]
    grad_value = grad_value.astype(jnp.float32) + dead_part[:, width:]

    selection = slot_selection(plan_row, member, capacity_blocks, rows)
    slot_cots = jnp.dot(
        selection.astype(jnp.bfloat16), dead_cots, preferred_element_type=jnp.float32
    ).astype(jnp.bfloat16)
    slot_scale = jnp.sum(selection * jnp.reshape(dead_scale, (1, rows)), axis=1, keepdims=True)
    slot_cots, _ = lax.optimization_barrier((slot_cots, (key_parts, value_parts)))
    across, straight = feature_halves(slot_cots, slot_scale, w_key[0], w_value[0], side)
    across = moved(across, lambda x, z, s, t: (x, z, s - 1, 1 - t))
    straight = moved(straight, lambda x, z, s, t: (x, z, s - 1, t))
    feature = straight.astype(jnp.float32) + across.astype(jnp.float32)
    spill_grad = (norm_gain * feature).astype(jnp.bfloat16)

    return grad_key[None], grad_value[None], stream_grad[None], spill_grad[None]


def solution(mesh):
    return jax.shard_map(
        on_device,
        mesh=mesh,
        in_specs=(
            P("pipe", "dp", "tensor"),
            P("pipe", "dp", "tensor"),
            P("tensor"),
            P("pipe", None, "tensor"),
            P("pipe", None, "tensor"),
            P("pipe", "dp", "tensor"),
            P("pipe", "dp", "tensor"),
            P("pipe", "dp", "tensor"),
            P("pipe", "dp", "tensor"),
            P("pipe", None),
            P(),
            P(),
        ),
        out_specs=(
            P("pipe", "dp", "tensor"),
            P("pipe", "dp", "tensor"),
            P("pipe", "dp", "tensor"),
            P("pipe", "dp", "tensor"),
        ),
        check_vma=False,
    )
```

```python
import itertools
import math

import jax
import jax.numpy as jnp
from jax import lax
from jax.experimental import pallas as pl
from jax.experimental.pallas import tpu as pltpu
from jax.sharding import PartitionSpec as P

D = 8192
HEAD = 128
BLOCK = 8
RING = 4
SECTIONS = 4

EPSILON = 1e-05
ROPE_BASE = 500000.0

AXES = ("dp", "pipe", "tensor")


def moved(block, rule):
    route = []
    for x, z, s, t in itertools.product(range(RING), range(RING), range(SECTIONS), range(2)):
        target = rule(x, z, s, t)
        if target is not None:
            a, b, c, d = target
            there = ((a % RING * RING + b % RING) * SECTIONS + c % SECTIONS) * 2 + d % 2
            route.append((((x * RING + z) * SECTIONS + s) * 2 + t, there))
    return lax.ppermute(block, AXES, route)


def both_sides(squares):
    return squares + moved(squares, lambda x, z, s, t: (x, z, s, 1 - t))


def frequencies():
    index_half = jnp.arange(HEAD // 2, dtype=jnp.float32)
    return jnp.exp(-(2.0 * index_half / HEAD) * math.log(ROPE_BASE))


def angles_of(position):
    angles = position.astype(jnp.float32)[:, None] * jnp.tile(frequencies(), 2)[None, :]
    sign = jnp.where(jnp.arange(HEAD) < HEAD // 2, 1.0, -1.0)
    return jnp.cos(angles), jnp.sin(angles) * sign


def derotate_kernel(key, value, cosine, sine, out):
    width = key.shape[1]
    for start in range(0, width, HEAD):
        head = key[:, start : start + HEAD].astype(jnp.float32)
        swapped = pltpu.roll(head, HEAD // 2, 1)
        out[:, start : start + HEAD] = (head * cosine[...] + swapped * sine[...]).astype(out.dtype)
    out[:, width:] = value[...]


def derotate(key, value, position):
    cosine, sine = angles_of(position)
    return pl.pallas_call(
        derotate_kernel,
        out_shape=jax.ShapeDtypeStruct((key.shape[0], 2 * key.shape[1]), jnp.bfloat16),
    )(key, value, cosine, sine)


def slot_selection(plan_row, owner, capacity_blocks, rows):
    block_count = plan_row.shape[0]
    block_ids = jnp.arange(block_count, dtype=jnp.int32)
    same_owner = plan_row[:, None] == plan_row[None, :]
    earlier = block_ids[None, :] < block_ids[:, None]
    block_rank = jnp.sum(jnp.where(same_owner & earlier, 1, 0), axis=1).astype(jnp.int32)
    slot_of_block = jnp.where(plan_row == owner, block_rank, -1)
    slot_of_row = jnp.repeat(slot_of_block, BLOCK) * BLOCK + jnp.tile(
        jnp.arange(BLOCK, dtype=jnp.int32), block_count
    )
    slot_of_row = jnp.where(jnp.repeat(slot_of_block, BLOCK) < 0, -1, slot_of_row)
    slot_ids = jnp.arange(capacity_blocks * BLOCK, dtype=jnp.int32)
    return (slot_ids[:, None] == slot_of_row[None, :]).astype(jnp.float32)


NT = (((1,), (1,)), ((), ()))
TN = (((0,), (0,)), ((), ()))
TILE = 1024


def feature_kernel(half, cots, scale, w_key, w_value, across, straight):
    rows, width = cots.shape[0], w_key.shape[1]
    tiles = D // 2 // TILE

    def step(key_tile, value_tile, out):
        total = lax.dot_general(
            cots[:, :width], key_tile[...], NT, preferred_element_type=jnp.float32
        )
        total = total + lax.dot_general(
            cots[:, width:], value_tile[...], NT, preferred_element_type=jnp.float32
        )
        out[...] = (total * scale[...]).astype(out.dtype)

    for side, out in ((1 - half[0], across), (half[0], straight)):
        weights = pl.BlockSpec((TILE, width), lambda i, side=side: (side * tiles + i, 0))
        pltpu.emit_pipeline(
            step,
            grid=(tiles,),
            in_specs=[weights, weights],
            out_specs=[pl.BlockSpec((rows, TILE), lambda i: (0, i))],
        )(w_key, w_value, out)


def feature_halves(cots, scale, w_key, w_value, half):
    rows = cots.shape[0]
    result = jax.ShapeDtypeStruct((rows, D // 2), jnp.bfloat16)
    return pl.pallas_call(
        feature_kernel,
        out_shape=(result, result),
        in_specs=[
            pl.BlockSpec(memory_space=pltpu.SMEM),
            pl.BlockSpec(memory_space=pltpu.VMEM),
            pl.BlockSpec(memory_space=pltpu.VMEM),
            pl.BlockSpec(memory_space=pltpu.HBM),
            pl.BlockSpec(memory_space=pltpu.HBM),
        ],
        out_specs=(pl.BlockSpec(memory_space=pltpu.HBM), pl.BlockSpec(memory_space=pltpu.HBM)),
        compiler_params=pltpu.CompilerParams(vmem_limit_bytes=32 * 1024 * 1024),
    )(
        jnp.reshape(half, (1,)),
        cots,
        scale,
        pltpu.with_memory_space_constraint(w_key, pltpu.HBM),
        pltpu.with_memory_space_constraint(w_value, pltpu.HBM),
    )


def product_kernel(places, *refs):
    *operands, out = refs
    count = len(operands) // 2
    total = None
    for lhs, rhs in zip(operands[:count], operands[count:]):
        lhs = lhs[...].reshape(-1, lhs.shape[-1])
        rhs = rhs[...].reshape(-1, rhs.shape[-1])
        part = lax.dot_general(lhs, rhs, TN, preferred_element_type=jnp.float32)
        total = part if total is None else total + part
    out[0] = total.astype(out.dtype)


def products(gathered, block, halves, heads):
    left = [
        pl.BlockSpec((g.shape[0], g.shape[1], block), lambda i, at: (0, 0, at[0, i])) for g in gathered
    ]
    right = [
        pl.BlockSpec((g.shape[0], g.shape[1], block), lambda i, at: (0, 0, at[1, i])) for g in gathered
    ]
    places = jnp.stack([jnp.stack(halves), jnp.stack(heads) + 2]).astype(jnp.int32)
    return pl.pallas_call(
        product_kernel,
        out_shape=jax.ShapeDtypeStruct((RING, block, block), jnp.bfloat16),
        grid_spec=pltpu.PrefetchScalarGridSpec(
            num_scalar_prefetch=1,
            grid=(RING,),
            in_specs=left + right,
            out_specs=pl.BlockSpec((1, block, block), lambda i, at: (i, 0, 0)),
        ),
        compiler_params=pltpu.CompilerParams(vmem_limit_bytes=32 * 1024 * 1024),
    )(places, *gathered, *gathered)


def pack_kernel(saved, out):
    piece = out.shape[-1]
    for half in range(2):
        for z in range(RING):
            start = (2 * z + half) * piece
            out[half, 0, z] = saved[:, start : start + piece]


def packed(saved, replicas):
    rows, features = saved.shape
    piece = features // replicas
    out = pl.pallas_call(
        pack_kernel,
        out_shape=jax.ShapeDtypeStruct((2, 2, RING, rows, piece), saved.dtype),
        grid=(2,),
        in_specs=[pl.BlockSpec((rows, features // 2), lambda i: (0, i))],
        out_specs=pl.BlockSpec((2, 1, RING, rows, piece), lambda i: (0, i, 0, 0, 0)),
    )(saved)
    return out.reshape(replicas, rows, piece)


def on_device(
    stream,
    backup_stream,
    norm_gain,
    w_key,
    w_value,
    key_cot,
    value_cot,
    backup_key_cot,
    backup_value_cot,
    positions,
    failed,
    reroute_plan,
):
    section = lax.axis_index("pipe")
    member = lax.axis_index("dp")
    side = lax.axis_index("tensor")
    replicas = lax.axis_size("dp")
    at_x, at_z = member // RING, member % RING
    fallen = failed[section]
    plan_row = reroute_plan[section]
    rows = stream.shape[1]
    capacity_blocks = 2 * ((plan_row.shape[0] + replicas - 2) // (replicas - 1))
    width = w_key.shape[2]

    keeper = (fallen + 1) % replicas
    fourth = stream.shape[2] // RING
    block = fourth // 2
    piece = block // 2
    share = rows // replicas

    saved = backup_stream[0]
    saved_cots = jnp.concatenate([backup_key_cot[0], backup_value_cot[0]], axis=1)
    share_rows = lax.all_to_all(saved_cots.reshape(replicas, share, -1), "dp", 0, 0)
    share_rows = lax.dynamic_index_in_dim(share_rows, keeper, 0, keepdims=False)

    own_positions = lax.dynamic_slice_in_dim(positions[0], member * rows, rows, 0)
    cots = derotate(key_cot[0], value_cot[0], own_positions)
    near = moved(cots, lambda x, z, s, t: (x, z, s - 1, t))
    far = moved(cots, lambda x, z, s, t: (x, z, s - 1, 1 - t))

    values = stream[0].astype(jnp.float32)
    saved_values = saved.astype(jnp.float32)
    squares = both_sides(
        jnp.concatenate([jnp.sum(values * values, axis=1), jnp.sum(saved_values * saved_values, axis=1)])
    )
    scales = lax.rsqrt(squares / D + EPSILON)
    own_scale = scales[:rows, None]
    normed = (values * own_scale * norm_gain).astype(jnp.bfloat16)

    saved_scale = scales[rows:]
    scale_high = saved_scale.astype(jnp.bfloat16)
    scale_low = (saved_scale - scale_high.astype(jnp.float32)).astype(jnp.bfloat16)
    factors = jnp.concatenate([scale_high.reshape(share, -1), scale_low.reshape(share, -1)], axis=1)
    factors = jnp.pad(factors, ((0, 0), (0, HEAD - factors.shape[1])))
    shares = jnp.concatenate([share_rows, factors], axis=1)
    shares = lax.all_to_all(jnp.broadcast_to(shares, (replicas, *shares.shape)), "dp", 0, 0)

    steps = (2, 1, 3, 0)

    def along_x(tile, step):
        return moved(tile, lambda x, z, s, t: (x + step, z, s, t)) if step else tile

    def along_z(tile, step):
        return moved(tile, lambda x, z, s, t: (x, z + step, s, t)) if step else tile

    value_tiles, key_tiles = [], []
    for step in steps:
        there = (at_x + step) % RING
        start = (2 * (there % 2) + there // 2) * fourth
        value_tiles.append(
            jnp.concatenate(
                [lax.dynamic_slice_in_dim(normed, start, fourth, 1), near[:, width:], far[:, width:]],
                axis=1,
            )
        )
        start = (at_z + step) % RING * block
        key_tiles.append(
            jnp.concatenate(
                [
                    lax.dynamic_slice_in_dim(normed, start, block, 1),
                    lax.dynamic_slice_in_dim(normed, RING * block + start, block, 1),
                    near[:, :width],
                    far[:, :width],
                ],
                axis=1,
            )
        )

    saved_pieces, shares, _ = lax.optimization_barrier(
        (packed(saved, replicas), shares, (value_tiles, key_tiles))
    )
    dead = lax.all_to_all(saved_pieces, "dp", 0, 0)

    dead_raw = shares[:, :, : 2 * width].reshape(rows, 2 * width)
    factors = lax.dynamic_index_in_dim(shares[:, :, 2 * width :], keeper, 0, keepdims=False)
    factors = factors.astype(jnp.float32)
    dead_scale = (factors[:, :share] + factors[:, share : 2 * share]).reshape(rows)[:, None]
    dead_positions = lax.dynamic_slice_in_dim(positions[0], fallen * rows, rows, 0)
    dead_cots = derotate(dead_raw[:, :width], dead_raw[:, width:], dead_positions)

    selection = slot_selection(plan_row, member, capacity_blocks, rows)
    slot_cots = jnp.dot(
        selection.astype(jnp.bfloat16), dead_cots, preferred_element_type=jnp.float32
    ).astype(jnp.bfloat16)
    slot_scale = jnp.sum(selection * jnp.reshape(dead_scale, (1, rows)), axis=1, keepdims=True)
    across, straight = feature_halves(
        jnp.concatenate([cots, slot_cots], axis=0),
        jnp.concatenate([jnp.ones((rows, 1), jnp.float32), slot_scale], axis=0),
        w_key[0],
        w_value[0],
        side,
    )
    value_tiles[0], _ = lax.optimization_barrier((value_tiles[0], (across, straight)))
    across = moved(across, lambda x, z, s, t: (x, z, s - 1, 1 - t))
    straight = moved(straight, lambda x, z, s, t: (x, z, s - 1, t))

    key_rows = [along_z(tile, step)[None] for tile, step in zip(key_tiles, steps)]
    value_rows = [along_x(tile, step)[None] for tile, step in zip(value_tiles, steps)]

    there = [(at_z + step) % RING for step in steps]
    value_parts = products(
        value_rows, block, [r % 2 for r in there], [(r // 2) ^ (at_x // 2) for r in there]
    )
    value_total = sum(
        along_z(value_parts[place], step).astype(jnp.float32) for place, step in enumerate(steps)
    )
    grad_value = moved(
        value_total.astype(jnp.bfloat16),
        lambda x, z, s, t: (2 * t + x % 2, 2 * (x // 2) + z % 2, s + 1, t ^ (z // 2) ^ (x // 2)),
    )
    static = [jnp.int32(r) for r in range(RING)]
    key_parts = products(key_rows, block, [r % 2 for r in static], [(r // 2) ^ side for r in static])
    x_rings = [[RING * x + z for x in range(RING)] for z in range(RING)]
    parts = lax.all_to_all(key_parts, "dp", 0, 0, axis_index_groups=x_rings)
    key_total = jnp.sum(parts.astype(jnp.float32), axis=0).astype(jnp.bfloat16)
    key_total, across, straight = lax.optimization_barrier((key_total, across, straight))
    grad_key = moved(key_total, lambda x, z, s, t: (2 * t + x % 2, z, s + 1, x // 2))

    feature = norm_gain * (straight.astype(jnp.float32) + across.astype(jnp.float32))
    stream_grad = (own_scale * feature[:rows]).astype(jnp.bfloat16)
    spill_grad = feature[rows:].astype(jnp.bfloat16)

    start = (at_x % 2 * RING + at_z) * block + at_x // 2 * piece
    dead = lax.dynamic_index_in_dim(dead, keeper, 0, keepdims=False)
    dead_piece = (
        dead.astype(jnp.float32) * dead_scale * lax.dynamic_slice_in_dim(norm_gain, start, piece, 0)
    ).astype(jnp.bfloat16)
    sent = moved(
        dead_piece, lambda x, z, s, t: (x, z, s, 1 - t) if x // 2 == t else (x + 2, z, s, t)
    )
    lent = moved(dead_piece, lambda x, z, s, t: None if x // 2 == t else (x + 2, z, s, 1 - t))
    home = at_x // 2
    same = jnp.where(home == side, dead_piece, sent)
    other = jnp.where(home == side, sent, lent)
    dead_block = jnp.concatenate(
        [jnp.where(home == 0, same, other), jnp.where(home == 0, other, same)], axis=1
    )
    dead_part = lax.dot_general(dead_block, dead_cots, TN, preferred_element_type=jnp.float32)
    grad_key = grad_key.astype(jnp.float32) + dead_part[:, :width]
    grad_value = grad_value.astype(jnp.float32) + dead_part[:, width:]

    return grad_key[None], grad_value[None], stream_grad[None], spill_grad[None]


def solution(mesh):
    return jax.shard_map(
        on_device,
        mesh=mesh,
        in_specs=(
            P("pipe", "dp", "tensor"),
            P("pipe", "dp", "tensor"),
            P("tensor"),
            P("pipe", None, "tensor"),
            P("pipe", None, "tensor"),
            P("pipe", "dp", "tensor"),
            P("pipe", "dp", "tensor"),
            P("pipe", "dp", "tensor"),
            P("pipe", "dp", "tensor"),
            P("pipe", None),
            P(),
            P(),
        ),
        out_specs=(
            P("pipe", "dp", "tensor"),
            P("pipe", "dp", "tensor"),
            P("pipe", "dp", "tensor"),
            P("pipe", "dp", "tensor"),
        ),
        check_vma=False,
    )
```

```python
import itertools
import math

import jax
import jax.numpy as jnp
from jax import lax
from jax.experimental import pallas as pl
from jax.experimental.pallas import tpu as pltpu
from jax.sharding import PartitionSpec as P

D = 8192
HEAD = 128
BLOCK = 8
RING = 4
SECTIONS = 4

EPSILON = 1e-05
ROPE_BASE = 500000.0

AXES = ("dp", "pipe", "tensor")


def moved(block, rule):
    route = []
    for x, z, s, t in itertools.product(range(RING), range(RING), range(SECTIONS), range(2)):
        target = rule(x, z, s, t)
        if target is not None:
            a, b, c, d = target
            there = ((a % RING * RING + b % RING) * SECTIONS + c % SECTIONS) * 2 + d % 2
            route.append((((x * RING + z) * SECTIONS + s) * 2 + t, there))
    return lax.ppermute(block, AXES, route)


def both_sides(squares):
    return squares + moved(squares, lambda x, z, s, t: (x, z, s, 1 - t))


def frequencies():
    index_half = jnp.arange(HEAD // 2, dtype=jnp.float32)
    return jnp.exp(-(2.0 * index_half / HEAD) * math.log(ROPE_BASE))


def angles_of(position):
    angles = position.astype(jnp.float32)[:, None] * jnp.tile(frequencies(), 2)[None, :]
    sign = jnp.where(jnp.arange(HEAD) < HEAD // 2, 1.0, -1.0)
    return jnp.cos(angles), jnp.sin(angles) * sign


def derotate_kernel(key, value, cosine, sine, out):
    width = key.shape[1]
    for start in range(0, width, HEAD):
        head = key[:, start : start + HEAD].astype(jnp.float32)
        swapped = pltpu.roll(head, HEAD // 2, 1)
        out[:, start : start + HEAD] = (head * cosine[...] + swapped * sine[...]).astype(out.dtype)
    out[:, width:] = value[...]


def derotate(key, value, position):
    cosine, sine = angles_of(position)
    return pl.pallas_call(
        derotate_kernel,
        out_shape=jax.ShapeDtypeStruct((key.shape[0], 2 * key.shape[1]), jnp.bfloat16),
    )(key, value, cosine, sine)


def slot_selection(plan_row, owner, capacity_blocks, rows):
    block_count = plan_row.shape[0]
    block_ids = jnp.arange(block_count, dtype=jnp.int32)
    same_owner = plan_row[:, None] == plan_row[None, :]
    earlier = block_ids[None, :] < block_ids[:, None]
    block_rank = jnp.sum(jnp.where(same_owner & earlier, 1, 0), axis=1).astype(jnp.int32)
    slot_of_block = jnp.where(plan_row == owner, block_rank, -1)
    slot_of_row = jnp.repeat(slot_of_block, BLOCK) * BLOCK + jnp.tile(
        jnp.arange(BLOCK, dtype=jnp.int32), block_count
    )
    slot_of_row = jnp.where(jnp.repeat(slot_of_block, BLOCK) < 0, -1, slot_of_row)
    slot_ids = jnp.arange(capacity_blocks * BLOCK, dtype=jnp.int32)
    return (slot_ids[:, None] == slot_of_row[None, :]).astype(jnp.float32)


NT = (((1,), (1,)), ((), ()))
TN = (((0,), (0,)), ((), ()))
TILE = 1024


def feature_kernel(half, cots, scale, w_key, w_value, across, straight):
    rows, width = cots.shape[0], w_key.shape[1]
    tiles = D // 2 // TILE

    def step(key_tile, value_tile, out):
        total = lax.dot_general(
            cots[:, :width], key_tile[...], NT, preferred_element_type=jnp.float32
        )
        total = total + lax.dot_general(
            cots[:, width:], value_tile[...], NT, preferred_element_type=jnp.float32
        )
        out[...] = (total * scale[...]).astype(out.dtype)

    for side, out in ((1 - half[0], across), (half[0], straight)):
        weights = pl.BlockSpec((TILE, width), lambda i, side=side: (side * tiles + i, 0))
        pltpu.emit_pipeline(
            step,
            grid=(tiles,),
            in_specs=[weights, weights],
            out_specs=[pl.BlockSpec((rows, TILE), lambda i: (0, i))],
        )(w_key, w_value, out)


def feature_halves(cots, scale, w_key, w_value, half):
    rows = cots.shape[0]
    result = jax.ShapeDtypeStruct((rows, D // 2), jnp.bfloat16)
    return pl.pallas_call(
        feature_kernel,
        out_shape=(result, result),
        in_specs=[
            pl.BlockSpec(memory_space=pltpu.SMEM),
            pl.BlockSpec(memory_space=pltpu.VMEM),
            pl.BlockSpec(memory_space=pltpu.VMEM),
            pl.BlockSpec(memory_space=pltpu.HBM),
            pl.BlockSpec(memory_space=pltpu.HBM),
        ],
        out_specs=(pl.BlockSpec(memory_space=pltpu.HBM), pl.BlockSpec(memory_space=pltpu.HBM)),
        compiler_params=pltpu.CompilerParams(vmem_limit_bytes=32 * 1024 * 1024),
    )(
        jnp.reshape(half, (1,)),
        cots,
        scale,
        pltpu.with_memory_space_constraint(w_key, pltpu.HBM),
        pltpu.with_memory_space_constraint(w_value, pltpu.HBM),
    )


def product_kernel(places, *refs):
    *operands, out = refs
    count = len(operands) // 2
    total = None
    for lhs, rhs in zip(operands[:count], operands[count:]):
        lhs = lhs[...].reshape(-1, lhs.shape[-1])
        rhs = rhs[...].reshape(-1, rhs.shape[-1])
        part = lax.dot_general(lhs, rhs, TN, preferred_element_type=jnp.float32)
        total = part if total is None else total + part
    out[0] = total.astype(out.dtype)


def products(gathered, block, halves, heads):
    left = [
        pl.BlockSpec((g.shape[0], g.shape[1], block), lambda i, at: (0, 0, at[0, i])) for g in gathered
    ]
    right = [
        pl.BlockSpec((g.shape[0], g.shape[1], block), lambda i, at: (0, 0, at[1, i])) for g in gathered
    ]
    places = jnp.stack([jnp.stack(halves), jnp.stack(heads) + 2]).astype(jnp.int32)
    return pl.pallas_call(
        product_kernel,
        out_shape=jax.ShapeDtypeStruct((RING, block, block), jnp.bfloat16),
        grid_spec=pltpu.PrefetchScalarGridSpec(
            num_scalar_prefetch=1,
            grid=(RING,),
            in_specs=left + right,
            out_specs=pl.BlockSpec((1, block, block), lambda i, at: (i, 0, 0)),
        ),
        compiler_params=pltpu.CompilerParams(vmem_limit_bytes=32 * 1024 * 1024),
    )(places, *gathered, *gathered)


def pack_kernel(saved, key, value, out):
    rows, piece = saved.shape[0], out.shape[-1]
    share = key.shape[0] // (4 * RING)
    for half in range(2):
        for z in range(RING):
            start = (2 * z + half) * piece
            out[half, 0, z, :rows] = saved[:, start : start + piece]
            at = rows
            mine = pl.ds(((2 * half + pl.program_id(0)) * RING + z) * share, share)
            for source in (key, value):
                for column in range(0, source.shape[1], piece):
                    out[half, 0, z, at : at + share] = source[mine, column : column + piece]
                    at += share


def packed(saved, key, value, replicas):
    rows, features = saved.shape
    piece, share = features // replicas, rows // replicas
    height = rows + 2 * key.shape[1] // piece * share
    whole = pl.BlockSpec(key.shape, lambda i: (0, 0))
    out = pl.pallas_call(
        pack_kernel,
        out_shape=jax.ShapeDtypeStruct((2, 2, RING, height, piece), saved.dtype),
        grid=(2,),
        in_specs=[pl.BlockSpec((rows, features // 2), lambda i: (0, i)), whole, whole],
        out_specs=pl.BlockSpec((2, 1, RING, height, piece), lambda i: (0, i, 0, 0, 0)),
    )(saved, key, value)
    return out.reshape(replicas, height, piece)


def on_device(
    stream,
    backup_stream,
    norm_gain,
    w_key,
    w_value,
    key_cot,
    value_cot,
    backup_key_cot,
    backup_value_cot,
    positions,
    failed,
    reroute_plan,
):
    section = lax.axis_index("pipe")
    member = lax.axis_index("dp")
    side = lax.axis_index("tensor")
    replicas = lax.axis_size("dp")
    at_x, at_z = member // RING, member % RING
    fallen = failed[section]
    plan_row = reroute_plan[section]
    rows = stream.shape[1]
    capacity_blocks = 2 * ((plan_row.shape[0] + replicas - 2) // (replicas - 1))
    width = w_key.shape[2]

    keeper = (fallen + 1) % replicas
    fourth = stream.shape[2] // RING
    block = fourth // 2
    piece = block // 2
    share = rows // replicas

    saved = backup_stream[0]
    dead = lax.all_to_all(
        packed(saved, backup_key_cot[0], backup_value_cot[0], replicas), "dp", 0, 0
    )

    own_positions = lax.dynamic_slice_in_dim(positions[0], member * rows, rows, 0)
    cots = derotate(key_cot[0], value_cot[0], own_positions)
    near = moved(cots, lambda x, z, s, t: (x, z, s - 1, t))
    far = moved(cots, lambda x, z, s, t: (x, z, s - 1, 1 - t))

    other_gain = moved(norm_gain, lambda x, z, s, t: (x, z, s, 1 - t))

    values = stream[0].astype(jnp.float32)
    saved_values = saved.astype(jnp.float32)
    squares = both_sides(
        jnp.concatenate([jnp.sum(values * values, axis=1), jnp.sum(saved_values * saved_values, axis=1)])
    )
    scales = lax.rsqrt(squares / D + EPSILON)
    own_scale = scales[:rows, None]
    own_scale, other_gain = lax.optimization_barrier((own_scale, other_gain))
    normed = (values * own_scale * norm_gain).astype(jnp.bfloat16)

    steps = (2, 1, 3, 0)

    def along_x(tile, step):
        return moved(tile, lambda x, z, s, t: (x + step, z, s, t)) if step else tile

    def along_z(tile, step):
        return moved(tile, lambda x, z, s, t: (x, z + step, s, t)) if step else tile

    value_tiles, key_tiles = [], []
    for step in steps:
        there = (at_x + step) % RING
        start = (2 * (there % 2) + there // 2) * fourth
        value_tiles.append(
            jnp.concatenate(
                [lax.dynamic_slice_in_dim(normed, start, fourth, 1), near[:, width:], far[:, width:]],
                axis=1,
            )
        )
        start = (at_z + step) % RING * block
        key_tiles.append(
            jnp.concatenate(
                [
                    lax.dynamic_slice_in_dim(normed, start, block, 1),
                    lax.dynamic_slice_in_dim(normed, RING * block + start, block, 1),
                    near[:, :width],
                    far[:, :width],
                ],
                axis=1,
            )
        )

    value_tiles, key_tiles = lax.optimization_barrier((value_tiles, key_tiles))
    dead, late_cots, _ = lax.optimization_barrier((dead, cots, (value_tiles, key_tiles)))
    saved_scale = scales[rows:]
    scale_high = saved_scale.astype(jnp.bfloat16)
    scale_low = (saved_scale - scale_high.astype(jnp.float32)).astype(jnp.bfloat16)
    factors = jnp.concatenate([scale_high.reshape(share, -1), scale_low.reshape(share, -1)], axis=1)
    factors = jnp.pad(factors, ((0, 0), (0, HEAD - factors.shape[1])))
    dead = lax.dynamic_index_in_dim(dead, keeper, 0, keepdims=False)
    share_rows = dead[rows:].reshape(-1, share, piece).transpose(1, 0, 2).reshape(share, -1)
    shares = jnp.concatenate([share_rows, factors], axis=1)
    shares = lax.all_to_all(jnp.broadcast_to(shares, (replicas, *shares.shape)), "dp", 0, 0)

    across, straight = feature_halves(
        late_cots, jnp.ones((rows, 1), jnp.float32), w_key[0], w_value[0], side
    )
    value_tiles[2], _ = lax.optimization_barrier((value_tiles[2], (across, straight)))
    across = moved(across, lambda x, z, s, t: (x, z, s - 1, 1 - t))
    straight = moved(straight, lambda x, z, s, t: (x, z, s - 1, t))

    key_rows = [along_z(tile, step)[None] for tile, step in zip(key_tiles, steps)]
    value_rows = [along_x(tile, step)[None] for tile, step in zip(value_tiles, steps)]

    there = [(at_z + step) % RING for step in steps]
    dead_piece = dead[:rows]
    sent = moved(
        dead_piece, lambda x, z, s, t: (x, z, s, 1 - t) if x // 2 == t else (x + 2, z, s, t)
    )
    lent = moved(dead_piece, lambda x, z, s, t: None if x // 2 == t else (x + 2, z, s, 1 - t))
    value_rows, key_rows, shares, sent, lent = lax.optimization_barrier(
        (value_rows, key_rows, shares, sent, lent)
    )
    value_parts = products(
        value_rows, block, [r % 2 for r in there], [(r // 2) ^ (at_x // 2) for r in there]
    )
    value_total = sum(
        along_z(value_parts[place], step).astype(jnp.float32) for place, step in enumerate(steps)
    )
    grad_value = moved(
        value_total.astype(jnp.bfloat16),
        lambda x, z, s, t: (2 * t + x % 2, 2 * (x // 2) + z % 2, s + 1, t ^ (z // 2) ^ (x // 2)),
    )
    static = [jnp.int32(r) for r in range(RING)]
    key_parts = products(key_rows, block, [r % 2 for r in static], [(r // 2) ^ side for r in static])
    x_rings = [[RING * x + z for x in range(RING)] for z in range(RING)]
    parts = lax.all_to_all(key_parts, "dp", 0, 0, axis_index_groups=x_rings)
    key_total = jnp.sum(parts.astype(jnp.float32), axis=0).astype(jnp.bfloat16)
    key_total, across, straight = lax.optimization_barrier((key_total, across, straight))
    grad_key = moved(key_total, lambda x, z, s, t: (2 * t + x % 2, z, s + 1, x // 2))

    feature = norm_gain * (straight.astype(jnp.float32) + across.astype(jnp.float32))
    stream_grad = (own_scale * feature).astype(jnp.bfloat16)

    dead_raw = shares[:, :, : 2 * width].reshape(rows, 2 * width)
    factors = lax.dynamic_index_in_dim(shares[:, :, 2 * width :], keeper, 0, keepdims=False)
    factors = factors.astype(jnp.float32)
    dead_scale = (factors[:, :share] + factors[:, share : 2 * share]).reshape(rows)[:, None]
    dead_positions = lax.dynamic_slice_in_dim(positions[0], fallen * rows, rows, 0)
    dead_cots = derotate(dead_raw[:, :width], dead_raw[:, width:], dead_positions)

    selection = slot_selection(plan_row, member, capacity_blocks, rows)
    slot_cots = jnp.dot(
        selection.astype(jnp.bfloat16), dead_cots, preferred_element_type=jnp.float32
    ).astype(jnp.bfloat16)
    slot_scale = jnp.sum(selection * jnp.reshape(dead_scale, (1, rows)), axis=1, keepdims=True)
    slot_cots, _ = lax.optimization_barrier((slot_cots, (key_parts, value_parts)))
    across, straight = feature_halves(slot_cots, slot_scale, w_key[0], w_value[0], side)
    across, straight, value_total = lax.optimization_barrier((across, straight, value_total))
    across = moved(across, lambda x, z, s, t: (x, z, s - 1, 1 - t))
    straight = moved(straight, lambda x, z, s, t: (x, z, s - 1, t))
    feature = straight.astype(jnp.float32) + across.astype(jnp.float32)
    spill_grad = (norm_gain * feature).astype(jnp.bfloat16)

    home = at_x // 2
    start = (at_x % 2 * RING + at_z) * block
    gain = jnp.where(
        home == side,
        lax.dynamic_slice_in_dim(norm_gain, start, block, 0),
        lax.dynamic_slice_in_dim(other_gain, start, block, 0),
    )
    same = jnp.where(home == side, dead_piece, sent)
    other = jnp.where(home == side, sent, lent)
    dead_block = jnp.concatenate(
        [jnp.where(home == 0, same, other), jnp.where(home == 0, other, same)], axis=1
    )
    dead_block = (dead_block.astype(jnp.float32) * dead_scale * gain).astype(jnp.bfloat16)
    dead_part = lax.dot_general(dead_block, dead_cots, TN, preferred_element_type=jnp.float32)
    grad_key = grad_key.astype(jnp.float32) + dead_part[:, :width]
    grad_value = grad_value.astype(jnp.float32) + dead_part[:, width:]

    return grad_key[None], grad_value[None], stream_grad[None], spill_grad[None]


def solution(mesh):
    return jax.shard_map(
        on_device,
        mesh=mesh,
        in_specs=(
            P("pipe", "dp", "tensor"),
            P("pipe", "dp", "tensor"),
            P("tensor"),
            P("pipe", None, "tensor"),
            P("pipe", None, "tensor"),
            P("pipe", "dp", "tensor"),
            P("pipe", "dp", "tensor"),
            P("pipe", "dp", "tensor"),
            P("pipe", "dp", "tensor"),
            P("pipe", None),
            P(),
            P(),
        ),
        out_specs=(
            P("pipe", "dp", "tensor"),
            P("pipe", "dp", "tensor"),
            P("pipe", "dp", "tensor"),
            P("pipe", "dp", "tensor"),
        ),
        check_vma=False,
    )
```

```python
import itertools
import math

import jax
import jax.numpy as jnp
from jax import lax
from jax.experimental import pallas as pl
from jax.experimental.pallas import tpu as pltpu
from jax.sharding import PartitionSpec as P

D = 8192
HEAD = 128
BLOCK = 8
RING = 4
SECTIONS = 4

EPSILON = 1e-05
ROPE_BASE = 500000.0

AXES = ("dp", "pipe", "tensor")


def moved(block, rule):
    route = []
    for x, z, s, t in itertools.product(range(RING), range(RING), range(SECTIONS), range(2)):
        target = rule(x, z, s, t)
        if target is not None:
            a, b, c, d = target
            there = ((a % RING * RING + b % RING) * SECTIONS + c % SECTIONS) * 2 + d % 2
            route.append((((x * RING + z) * SECTIONS + s) * 2 + t, there))
    return lax.ppermute(block, AXES, route)


def both_sides(squares):
    return squares + moved(squares, lambda x, z, s, t: (x, z, s, 1 - t))


def frequencies():
    index_half = jnp.arange(HEAD // 2, dtype=jnp.float32)
    return jnp.exp(-(2.0 * index_half / HEAD) * math.log(ROPE_BASE))


def angles_of(position):
    angles = position.astype(jnp.float32)[:, None] * jnp.tile(frequencies(), 2)[None, :]
    sign = jnp.where(jnp.arange(HEAD) < HEAD // 2, 1.0, -1.0)
    return jnp.cos(angles), jnp.sin(angles) * sign


def derotate_kernel(key, value, cosine, sine, out):
    width = key.shape[1]
    for start in range(0, width, HEAD):
        head = key[:, start : start + HEAD].astype(jnp.float32)
        swapped = pltpu.roll(head, HEAD // 2, 1)
        out[:, start : start + HEAD] = (head * cosine[...] + swapped * sine[...]).astype(out.dtype)
    out[:, width:] = value[...]


def derotate(key, value, position):
    cosine, sine = angles_of(position)
    return pl.pallas_call(
        derotate_kernel,
        out_shape=jax.ShapeDtypeStruct((key.shape[0], 2 * key.shape[1]), jnp.bfloat16),
    )(key, value, cosine, sine)


def slot_selection(plan_row, owner, capacity_blocks, rows):
    block_count = plan_row.shape[0]
    block_ids = jnp.arange(block_count, dtype=jnp.int32)
    same_owner = plan_row[:, None] == plan_row[None, :]
    earlier = block_ids[None, :] < block_ids[:, None]
    block_rank = jnp.sum(jnp.where(same_owner & earlier, 1, 0), axis=1).astype(jnp.int32)
    slot_of_block = jnp.where(plan_row == owner, block_rank, -1)
    slot_of_row = jnp.repeat(slot_of_block, BLOCK) * BLOCK + jnp.tile(
        jnp.arange(BLOCK, dtype=jnp.int32), block_count
    )
    slot_of_row = jnp.where(jnp.repeat(slot_of_block, BLOCK) < 0, -1, slot_of_row)
    slot_ids = jnp.arange(capacity_blocks * BLOCK, dtype=jnp.int32)
    return (slot_ids[:, None] == slot_of_row[None, :]).astype(jnp.float32)


NT = (((1,), (1,)), ((), ()))
TN = (((0,), (0,)), ((), ()))
TILE = 2048


def feature_kernel(half, cots, scale, w_key, w_value, across, straight):
    rows, width = cots.shape[0], w_key.shape[1]
    tiles = D // 2 // TILE

    def step(key_tile, value_tile, out):
        total = lax.dot_general(
            cots[:, :width], key_tile[...], NT, preferred_element_type=jnp.float32
        )
        total = total + lax.dot_general(
            cots[:, width:], value_tile[...], NT, preferred_element_type=jnp.float32
        )
        out[...] = (total * scale[...]).astype(out.dtype)

    for side, out in ((1 - half[0], across), (half[0], straight)):
        weights = pl.BlockSpec((TILE, width), lambda i, side=side: (side * tiles + i, 0))
        pltpu.emit_pipeline(
            step,
            grid=(tiles,),
            in_specs=[weights, weights],
            out_specs=[pl.BlockSpec((rows, TILE), lambda i: (0, i))],
        )(w_key, w_value, out)


def feature_halves(cots, scale, w_key, w_value, half):
    rows = cots.shape[0]
    result = jax.ShapeDtypeStruct((rows, D // 2), jnp.bfloat16)
    return pl.pallas_call(
        feature_kernel,
        out_shape=(result, result),
        in_specs=[
            pl.BlockSpec(memory_space=pltpu.SMEM),
            pl.BlockSpec(memory_space=pltpu.VMEM),
            pl.BlockSpec(memory_space=pltpu.VMEM),
            pl.BlockSpec(memory_space=pltpu.HBM),
            pl.BlockSpec(memory_space=pltpu.HBM),
        ],
        out_specs=(pl.BlockSpec(memory_space=pltpu.HBM), pl.BlockSpec(memory_space=pltpu.HBM)),
        compiler_params=pltpu.CompilerParams(vmem_limit_bytes=40 * 1024 * 1024),
    )(
        jnp.reshape(half, (1,)),
        cots,
        scale,
        pltpu.with_memory_space_constraint(w_key, pltpu.HBM),
        pltpu.with_memory_space_constraint(w_value, pltpu.HBM),
    )


def product_kernel(places, *refs):
    *operands, out = refs
    count = len(operands) // 2
    total = None
    for lhs, rhs in zip(operands[:count], operands[count:]):
        lhs = lhs[...].reshape(-1, lhs.shape[-1])
        rhs = rhs[...].reshape(-1, rhs.shape[-1])
        part = lax.dot_general(lhs, rhs, TN, preferred_element_type=jnp.float32)
        total = part if total is None else total + part
    out[0] = total.astype(out.dtype)


def products(gathered, block, halves, heads):
    left = [
        pl.BlockSpec((g.shape[0], g.shape[1], block), lambda i, at: (0, 0, at[0, i])) for g in gathered
    ]
    right = [
        pl.BlockSpec((g.shape[0], g.shape[1], block), lambda i, at: (0, 0, at[1, i])) for g in gathered
    ]
    places = jnp.stack([jnp.stack(halves), jnp.stack(heads) + 2]).astype(jnp.int32)
    return pl.pallas_call(
        product_kernel,
        out_shape=jax.ShapeDtypeStruct((RING, block, block), jnp.bfloat16),
        grid_spec=pltpu.PrefetchScalarGridSpec(
            num_scalar_prefetch=1,
            grid=(RING,),
            in_specs=left + right,
            out_specs=pl.BlockSpec((1, block, block), lambda i, at: (i, 0, 0)),
        ),
        compiler_params=pltpu.CompilerParams(vmem_limit_bytes=40 * 1024 * 1024),
    )(places, *gathered, *gathered)


def pack_kernel(saved, out):
    piece = out.shape[-1]
    for half in range(2):
        for z in range(RING):
            start = (2 * z + half) * piece
            out[half, 0, z] = saved[:, start : start + piece]


def packed(saved, replicas):
    rows, features = saved.shape
    piece = features // replicas
    out = pl.pallas_call(
        pack_kernel,
        out_shape=jax.ShapeDtypeStruct((2, 2, RING, rows, piece), saved.dtype),
        grid=(2,),
        in_specs=[pl.BlockSpec((rows, features // 2), lambda i: (0, i))],
        out_specs=pl.BlockSpec((2, 1, RING, rows, piece), lambda i: (0, i, 0, 0, 0)),
    )(saved)
    return out.reshape(replicas, rows, piece)


def on_device(
    stream,
    backup_stream,
    norm_gain,
    w_key,
    w_value,
    key_cot,
    value_cot,
    backup_key_cot,
    backup_value_cot,
    positions,
    failed,
    reroute_plan,
):
    section = lax.axis_index("pipe")
    member = lax.axis_index("dp")
    side = lax.axis_index("tensor")
    replicas = lax.axis_size("dp")
    at_x, at_z = member // RING, member % RING
    fallen = failed[section]
    plan_row = reroute_plan[section]
    rows = stream.shape[1]
    capacity_blocks = 2 * ((plan_row.shape[0] + replicas - 2) // (replicas - 1))
    width = w_key.shape[2]

    keeper = (fallen + 1) % replicas
    fourth = stream.shape[2] // RING
    block = fourth // 2
    piece = block // 2
    share = rows // replicas

    saved = backup_stream[0]
    saved_cots = jnp.concatenate([backup_key_cot[0], backup_value_cot[0]], axis=1)
    share_rows = lax.all_to_all(saved_cots.reshape(replicas, share, -1), "dp", 0, 0)
    share_rows = lax.dynamic_index_in_dim(share_rows, keeper, 0, keepdims=False)

    own_positions = lax.dynamic_slice_in_dim(positions[0], member * rows, rows, 0)
    cots = derotate(key_cot[0], value_cot[0], own_positions)
    near = moved(cots, lambda x, z, s, t: (x, z, s - 1, t))
    far = moved(cots, lambda x, z, s, t: (x, z, s - 1, 1 - t))

    values = stream[0].astype(jnp.float32)
    saved_values = saved.astype(jnp.float32)
    squares = both_sides(
        jnp.concatenate([jnp.sum(values * values, axis=1), jnp.sum(saved_values * saved_values, axis=1)])
    )
    scales = lax.rsqrt(squares / D + EPSILON)
    own_scale = scales[:rows, None]
    normed = (values * own_scale * norm_gain).astype(jnp.bfloat16)

    saved_scale = scales[rows:]
    scale_high = saved_scale.astype(jnp.bfloat16)
    scale_low = (saved_scale - scale_high.astype(jnp.float32)).astype(jnp.bfloat16)
    factors = jnp.concatenate([scale_high.reshape(share, -1), scale_low.reshape(share, -1)], axis=1)
    factors = jnp.pad(factors, ((0, 0), (0, HEAD - factors.shape[1])))
    shares = jnp.concatenate([share_rows, factors], axis=1)
    shares = lax.all_to_all(jnp.broadcast_to(shares, (replicas, *shares.shape)), "dp", 0, 0)

    steps = (2, 1, 3, 0)

    def along_x(tile, step):
        return moved(tile, lambda x, z, s, t: (x + step, z, s, t)) if step else tile

    def along_z(tile, step):
        return moved(tile, lambda x, z, s, t: (x, z + step, s, t)) if step else tile

    value_tiles, key_tiles = [], []
    for step in steps:
        there = (at_x + step) % RING
        start = (2 * (there % 2) + there // 2) * fourth
        value_tiles.append(
            jnp.concatenate(
                [lax.dynamic_slice_in_dim(normed, start, fourth, 1), near[:, width:], far[:, width:]],
                axis=1,
            )
        )
        start = (at_z + step) % RING * block
        key_tiles.append(
            jnp.concatenate(
                [
                    lax.dynamic_slice_in_dim(normed, start, block, 1),
                    lax.dynamic_slice_in_dim(normed, RING * block + start, block, 1),
                    near[:, :width],
                    far[:, :width],
                ],
                axis=1,
            )
        )

    saved_pieces, shares, _ = lax.optimization_barrier(
        (packed(saved, replicas), shares, (value_tiles, key_tiles))
    )
    dead = lax.all_to_all(saved_pieces, "dp", 0, 0)

    dead_raw = shares[:, :, : 2 * width].reshape(rows, 2 * width)
    factors = lax.dynamic_index_in_dim(shares[:, :, 2 * width :], keeper, 0, keepdims=False)
    factors = factors.astype(jnp.float32)
    dead_scale = (factors[:, :share] + factors[:, share : 2 * share]).reshape(rows)[:, None]
    dead_positions = lax.dynamic_slice_in_dim(positions[0], fallen * rows, rows, 0)
    dead_cots = derotate(dead_raw[:, :width], dead_raw[:, width:], dead_positions)

    selection = slot_selection(plan_row, member, capacity_blocks, rows)
    slot_cots = jnp.dot(
        selection.astype(jnp.bfloat16), dead_cots, preferred_element_type=jnp.float32
    ).astype(jnp.bfloat16)
    slot_scale = jnp.sum(selection * jnp.reshape(dead_scale, (1, rows)), axis=1, keepdims=True)
    across, straight = feature_halves(
        jnp.concatenate([cots, slot_cots], axis=0),
        jnp.concatenate([jnp.ones((rows, 1), jnp.float32), slot_scale], axis=0),
        w_key[0],
        w_value[0],
        side,
    )
    value_tiles[0], _ = lax.optimization_barrier((value_tiles[0], (across, straight)))
    across = moved(across, lambda x, z, s, t: (x, z, s - 1, 1 - t))
    straight = moved(straight, lambda x, z, s, t: (x, z, s - 1, t))

    key_rows = [along_z(tile, step)[None] for tile, step in zip(key_tiles, steps)]
    value_rows = [along_x(tile, step)[None] for tile, step in zip(value_tiles, steps)]

    there = [(at_z + step) % RING for step in steps]
    value_parts = products(
        value_rows, block, [r % 2 for r in there], [(r // 2) ^ (at_x // 2) for r in there]
    )
    value_total = sum(
        along_z(value_parts[place], step).astype(jnp.float32) for place, step in enumerate(steps)
    )
    grad_value = moved(
        value_total.astype(jnp.bfloat16),
        lambda x, z, s, t: (2 * t + x % 2, 2 * (x // 2) + z % 2, s + 1, t ^ (z // 2) ^ (x // 2)),
    )
    static = [jnp.int32(r) for r in range(RING)]
    key_parts = products(key_rows, block, [r % 2 for r in static], [(r // 2) ^ side for r in static])
    x_rings = [[RING * x + z for x in range(RING)] for z in range(RING)]
    parts = lax.all_to_all(key_parts, "dp", 0, 0, axis_index_groups=x_rings)
    key_total = jnp.sum(parts.astype(jnp.float32), axis=0).astype(jnp.bfloat16)
    grad_key = moved(key_total, lambda x, z, s, t: (2 * t + x % 2, z, s + 1, x // 2))

    feature = norm_gain * (straight.astype(jnp.float32) + across.astype(jnp.float32))
    stream_grad = (own_scale * feature[:rows]).astype(jnp.bfloat16)
    spill_grad = feature[rows:].astype(jnp.bfloat16)

    start = (at_x % 2 * RING + at_z) * block + at_x // 2 * piece
    dead = lax.dynamic_index_in_dim(dead, keeper, 0, keepdims=False)
    dead_piece = (
        dead.astype(jnp.float32) * dead_scale * lax.dynamic_slice_in_dim(norm_gain, start, piece, 0)
    ).astype(jnp.bfloat16)
    sent = moved(
        dead_piece, lambda x, z, s, t: (x, z, s, 1 - t) if x // 2 == t else (x + 2, z, s, t)
    )
    lent = moved(dead_piece, lambda x, z, s, t: None if x // 2 == t else (x + 2, z, s, 1 - t))
    home = at_x // 2
    same = jnp.where(home == side, dead_piece, sent)
    other = jnp.where(home == side, sent, lent)
    dead_block = jnp.concatenate(
        [jnp.where(home == 0, same, other), jnp.where(home == 0, other, same)], axis=1
    )
    dead_part = lax.dot_general(dead_block, dead_cots, TN, preferred_element_type=jnp.float32)
    grad_key = grad_key.astype(jnp.float32) + dead_part[:, :width]
    grad_value = grad_value.astype(jnp.float32) + dead_part[:, width:]

    return grad_key[None], grad_value[None], stream_grad[None], spill_grad[None]


def solution(mesh):
    return jax.shard_map(
        on_device,
        mesh=mesh,
        in_specs=(
            P("pipe", "dp", "tensor"),
            P("pipe", "dp", "tensor"),
            P("tensor"),
            P("pipe", None, "tensor"),
            P("pipe", None, "tensor"),
            P("pipe", "dp", "tensor"),
            P("pipe", "dp", "tensor"),
            P("pipe", "dp", "tensor"),
            P("pipe", "dp", "tensor"),
            P("pipe", None),
            P(),
            P(),
        ),
        out_specs=(
            P("pipe", "dp", "tensor"),
            P("pipe", "dp", "tensor"),
            P("pipe", "dp", "tensor"),
            P("pipe", "dp", "tensor"),
        ),
        check_vma=False,
    )
```
